32 devices in a mesh: grp: 2 (over x), tx: 16 (over z, y, core).
Axes of the slice: x: 2, y: 2, z: 4, core: 2. Of those that a mesh axis runs over, the one named last changes fastest.
Arguments:
- adjoint_in: float32 [3, 256, 256, 128], P(None, ('grp', 'tx')), parts along dimension 1, may hold values from -6 to 6
- forward_terms: bfloat16 [3, 3, 256, 256, 128], P(None, None, ('grp', 'tx')), parts along dimension 2, may hold values from -24 to 24
- log_conductivity: float32 [256, 256, 128], P(('grp', 'tx')), parts along dimension 0, may hold values from -1 to 1
- spacing: float32 [256, 256], P(('grp', 'tx')), parts along dimension 0, may hold values from 0.8 to 1.6
- residuals: float32 [35, 256, 256], P(None, ('grp', 'tx')), parts along dimension 1, may hold values from -6 to 6
- gate_index: int32 [6], P('grp'), parts along dimension 0, may hold values from 0 to 34
- counts: int32 [256, 256], P(('grp', 'tx')), parts along dimension 0, may hold values from 32 to 128, as said below
- voxel_column: int32 [256, 256], P(('grp', 'tx')), parts along dimension 0, may hold values from 0 to 8191, as said below
- voxel_model: float32 [64, 256, 128], P(('grp', 'tx')), parts along dimension 0, may hold values from -1 to 1
Outputs:
- adjoint_out: float32 [3, 256, 256, 128], P(None, ('grp', 'tx')), parts along dimension 1
- voxel_gradient: float32 [64, 256, 128], P(('grp', 'tx')), parts along dimension 0
The draws below stay inside these ranges and needn't reach their ends.
There are 2 independent parts, one for each index of `grp`. The reference program is written for one: setup_inputs(seed, part) draws one part's arguments, and reference() takes and returns one part's arrays. A program takes and returns all parts, laid end to end along the dimension named above; each array names one. Nothing has to cross between parts.
Inputs may be any that keep to these rules, and one draw needn't show every extreme that they name: `counts`: counts reach both ends of the range in every draw. `voxel_column`: voxel column v lies on tile v // 512. Among the 2048 columns of one tx index, at most 256 map to voxel columns of any one tile, and in every draw some tile receives exactly 256 columns from every tx index. Both ends of the range are reached in every draw.
All inputs are finite; a program needn't handle non-finite values.
Results may differ from the reference program's by a relative error of at most 0.0003.
Values sent between devices are 32-bit elements; how exact they have to be, the bound alone decides.
A program may use at most 128 MiB of HBM per device.

```python
import jax
import jax.numpy as jnp
from jax import lax

CX = 8
NY = 256
NZ = 128
G = 35
STEPS = 3
VCX = 2
VY = 256
NX = 128
VX = 32
N_TX = 16


def draw_counts(key, part):
    depths = jax.random.randint(key, (CX * N_TX * NY,), NZ // 4, NZ + 1)
    depths = depths.at[0].set(NZ).at[1].set(NZ // 4)
    return depths.reshape(CX * N_TX, NY).astype(jnp.int32)


def draw_voxel_column(key, part):
    column_count = CX * NY
    capacity = 2 * column_count // N_TX
    slot_count = N_TX * capacity
    voxel_count = VCX * VY
    crowded = jax.random.randint(jax.random.fold_in(key, 1), (), 0, N_TX)

    def draw_block(block_key):
        key_second, key_rank, key_mix, key_voxel = jax.random.split(block_key, 4)
        second = jax.random.randint(key_second, (), 0, N_TX)
        slot_rank = jax.random.permutation(key_rank, slot_count)
        slot_ids = jnp.arange(slot_count)
        slot_target = slot_ids // capacity
        forced = ((slot_ids == 0) | (slot_ids == slot_count - 1)).astype(jnp.int32)
        priority = slot_rank + 2 * slot_count * (slot_target != crowded).astype(jnp.int32) + slot_count * (slot_target != second).astype(jnp.int32) - 4 * slot_count * forced
        slot_order = jnp.argsort(priority)
        chosen = jax.random.permutation(key_mix, slot_order[:column_count])
        target = chosen // capacity
        local_voxel = jax.random.randint(key_voxel, (column_count,), 0, voxel_count)
        local_voxel = jnp.where(chosen == 0, 0, jnp.where(chosen == slot_count - 1, voxel_count - 1, local_voxel))
        return target * voxel_count + local_voxel
    block_keys = jax.random.split(jax.random.fold_in(key, 2), N_TX)
    return jax.vmap(draw_block)(block_keys).reshape(CX * N_TX, NY).astype(jnp.int32)


def steps_of(stream_key, extent, cuts, smallest, largest):
    loudness = 1.0
    for dim, blocks in cuts:
        steps = jax.random.uniform(jax.random.fold_in(jax.random.fold_in(stream_key, 6), dim), (blocks,), jnp.float32, smallest / len(cuts), largest / len(cuts))
        loudness = loudness * jnp.repeat(jnp.exp(steps), extent[dim] // blocks).reshape((-1,) + (1,) * (len(extent) - 1 - dim))
    return loudness


def gaussian(stream_key, dims, deviation, bound, cuts=(), kind=jnp.bfloat16):
    level = steps_of(stream_key, dims, cuts, -0.22, 0.18) if cuts else 1.0
    entries = jax.random.normal(stream_key, dims, jnp.float32) * deviation * level
    return jnp.minimum(jnp.maximum(entries, -bound), bound).astype(kind)


def setup_inputs(seed: int = 0, part: int = 0) -> dict:
    key_of = jax.random.split(jax.random.key(seed), 10)
    part_keys = jax.random.split(jax.random.fold_in(key_of[9], part), 10)
    return {
        "adjoint_in": gaussian(part_keys[0], (3, NX, NY, NZ), 1.0, 6.0, ((1, 16),), jnp.float32),
        "forward_terms": gaussian(part_keys[1], (STEPS, 3, NX, NY, NZ), 4.0, 24.0, ((2, 16),)),
        "log_conductivity": jnp.clip(jax.random.uniform(part_keys[2], (NX, NY, NZ), jnp.float32, -1.0, 1.0) * steps_of(part_keys[2], (NX, NY, NZ), ((0, 16),), -0.4, 0.0), -1.0, 1.0),
        "spacing": jnp.clip(0.8 + 0.8 * jax.random.uniform(part_keys[3], (NX, NY), jnp.float32) ** steps_of(part_keys[3], (NX, NY), ((0, 16),), -0.2, 0.2), 0.8, 1.6),
        "residuals": gaussian(part_keys[4], (G, NX, NY), 1.0, 6.0, ((1, 16),), jnp.float32),
        "gate_index": jax.random.randint(part_keys[5], (STEPS,), 0, G).astype(jnp.int32),
        "counts": draw_counts(jax.random.fold_in(jax.random.fold_in(key_of[9], part), 71), part),
        "voxel_column": draw_voxel_column(jax.random.fold_in(jax.random.fold_in(key_of[9], part), 71), part),
        "voxel_model": jnp.clip(jax.random.uniform(part_keys[8], (VX, VY, NZ), jnp.float32, -1.0, 1.0) * steps_of(part_keys[8], (VX, VY, NZ), ((0, 16),), -0.4, 0.0), -1.0, 1.0),
    }


def forward_diff(field, along):
    widths = [(0, 0)] * field.ndim
    widths[along] = (0, 1)
    padded = jnp.pad(field, widths)
    return lax.slice_in_dim(padded, 1, padded.shape[along], axis=along) - field


def backward_diff(field, along):
    widths = [(0, 0)] * field.ndim
    widths[along] = (1, 0)
    padded = jnp.pad(field, widths)
    return field - lax.slice_in_dim(padded, 0, field.shape[along], axis=along)


def curl_curl(field_x, field_y, field_z, inv_h):
    curl_x = forward_diff(field_z, 1) - forward_diff(field_y, 2) * inv_h
    curl_y = forward_diff(field_x, 2) * inv_h - forward_diff(field_z, 0)
    curl_z = forward_diff(field_y, 0) - forward_diff(field_x, 1)
    back_x = backward_diff(curl_z, 1) - backward_diff(curl_y, 2) * inv_h
    back_y = backward_diff(curl_x, 2) * inv_h - backward_diff(curl_z, 0)
    back_z = backward_diff(curl_y, 0) - backward_diff(curl_x, 1)
    return jnp.stack([back_x, back_y, back_z])


def reference(adjoint_in, forward_terms, log_conductivity, spacing, residuals, gate_index, counts, voxel_column, voxel_model):
    coefficient = 0.05 * jnp.exp(-0.7 * log_conductivity)
    inv_h = (1.0 / spacing)[:, :, None]
    sources = residuals[gate_index]
    adjoint = adjoint_in
    product_sum = jnp.zeros(log_conductivity.shape, jnp.float32)
    for step_index in range(STEPS):
        image = curl_curl(adjoint[0], adjoint[1], adjoint[2], inv_h)
        adjoint = adjoint - coefficient[None] * image
        adjoint = adjoint.at[2, :, :, NZ - 1].add(sources[step_index])
        product_sum = product_sum + jnp.sum(adjoint * forward_terms[step_index].astype(jnp.float32), axis=0)
    inside = jnp.arange(NZ, dtype=jnp.int32)[None, None, :] < counts[:, :, None]
    sensitivity = jnp.where(inside, -0.7 * coefficient * product_sum, 0.0)
    collected = jax.ops.segment_sum(sensitivity.reshape(NX * NY, NZ), voxel_column.reshape(NX * NY), num_segments=VX * VY)
    collected = collected.reshape(VX, VY, NZ)
    padded = jnp.pad(voxel_model, 1)
    laplace = 6.0 * voxel_model - padded[2:, 1:-1, 1:-1] - padded[:-2, 1:-1, 1:-1]
    laplace = laplace - padded[1:-1, 2:, 1:-1] - padded[1:-1, :-2, 1:-1]
    laplace = laplace - padded[1:-1, 1:-1, 2:] - padded[1:-1, 1:-1, :-2]
    return adjoint, collected + 0.1 * laplace
```

```python
import functools

import jax
import jax.numpy as jnp
from jax import lax
from jax.experimental import pallas as pl
from jax.experimental.pallas import tpu as pltpu
from jax.sharding import PartitionSpec as P

MESH = pl.DeviceIdType.MESH


def lane_index(shape):
    return lax.broadcasted_iota(jnp.int32, shape, 1)


def next_z(value):
    depth = value.shape[1]
    return jnp.where(lane_index(value.shape) < depth - 1, pltpu.roll(value, depth - 1, 1), 0.0)


def last_z(value):
    return jnp.where(lane_index(value.shape) > 0, pltpu.roll(value, 1, 1), 0.0)


def field_kernel(
    n,
    adj_ref,
    fwd_ref,
    logc_ref,
    spacing_ref,
    residual_ref,
    gate_ref,
    counts_ref,
    model_ref,
    out_ref,
    sens_ref,
    reg_ref,
    field,
    curl,
    coef,
    inv,
    total,
    terms,
    columns,
    from_low,
    from_high,
    to_high,
    model,
    model_low,
    model_high,
    local_sem,
    term_sem,
    send_up,
    send_down,
    recv_low,
    recv_high,
    model_send,
    model_recv,
):
    steps = fwd_ref.shape[0]
    cells, ny, nz = logc_ref.shape
    rows_v = model_ref.shape[0]
    grp, me = lax.axis_index("grp"), lax.axis_index("tx")
    low, high = lax.rem(me + n - 1, n), lax.rem(me + 1, n)
    has_low, has_high = me > 0, me < n - 1
    chunk = 64
    chunks = [(y, chunk) for y in range(0, ny, chunk)]

    load_last = pltpu.make_async_copy(
        adj_ref.at[:, pl.ds(cells - 1, 1)], field.at[:, pl.ds(cells - 1, 1), pl.ds(0, ny)], local_sem.at[0]
    )
    load_last.start()
    load_rest = pltpu.make_async_copy(
        adj_ref.at[:, pl.ds(0, cells - 1)], field.at[:, pl.ds(0, cells - 1), pl.ds(0, ny)], local_sem.at[1]
    )
    load_rest.start()
    load_coef = pltpu.make_async_copy(logc_ref, coef, local_sem.at[2])
    load_coef.start()
    load_terms = [pltpu.make_async_copy(fwd_ref.at[s], terms.at[s], term_sem.at[s]) for s in range(steps)]
    for copy in load_terms:
        copy.start()

    barrier = pltpu.get_barrier_semaphore()
    for neighbour in (low, high):
        pl.semaphore_signal(barrier, inc=1, device_id=(grp, neighbour), device_id_type=MESH)

    inverse = 1.0 / spacing_ref[...]
    depth_count = counts_ref[...].astype(jnp.float32)
    sources = [residual_ref[gate_ref[s]] for s in range(steps)]
    for y in range(0, ny, nz):
        parts = [v[:, y : y + nz] for v in [inverse, depth_count] + sources]
        parts.append(jnp.zeros((nz - cells * (2 + steps), nz), jnp.float32))
        columns[pl.ds(y, nz), :] = jnp.concatenate(parts, axis=0).T

    for x in range(cells):
        inv[x] = jnp.broadcast_to(columns[:, x : x + 1], (ny, nz))
        for a in range(3):
            field[a, x, pl.ds(ny, 8), :] = jnp.zeros((8, nz), jnp.float32)
            curl[a, x + 1, pl.ds(0, 8), :] = jnp.zeros((8, nz), jnp.float32)

    def copy_up(slot):
        return pltpu.make_async_remote_copy(
            src_ref=to_high.at[slot],
            dst_ref=from_low.at[slot],
            send_sem=send_up.at[slot],
            recv_sem=recv_low.at[slot],
            device_id=(grp, high),
            device_id_type=MESH,
        )

    def copy_down(slot):
        return pltpu.make_async_remote_copy(
            src_ref=field.at[pl.ds(1, 2), 0, pl.ds(0, ny)],
            dst_ref=from_high.at[slot],
            send_sem=send_down.at[slot],
            recv_sem=recv_high.at[slot],
            device_id=(grp, low),
            device_id_type=MESH,
        )

    def send_high(slot):
        x = cells - 1
        for y, size in chunks:
            e0, e1, e2 = (field[a, x, pl.ds(y, size), :] for a in range(3))
            e0y = field[0, x, pl.ds(y + 1, size), :]
            to_high[slot, 0, pl.ds(y, size), :] = inv[x, pl.ds(y, size), :] * (next_z(e0) - e0) + e2
            to_high[slot, 1, pl.ds(y, size), :] = (e0 - e0y) - e1

        @pl.when(has_high)
        def _():
            copy_up(slot).start()

    def send_low(slot):
        @pl.when(has_low)
        def _():
            copy_down(slot).start()

    def curl_row(x, next_row):
        for y, size in chunks:
            at = pl.ds(y, size)
            e0, e1, e2 = (field[a, x, at, :] for a in range(3))
            e0y, e2y = field[0, x, pl.ds(y + 1, size), :], field[2, x, pl.ds(y + 1, size), :]
            e1x, e2x = next_row(at)
            h = inv[x, at, :]
            to = pl.ds(y + 8, size)
            curl[0, x + 1, to, :] = (e2y - e2) - h * (next_z(e1) - e1)
            curl[1, x + 1, to, :] = h * (next_z(e0) - e0) - (e2x - e2)
            curl[2, x + 1, to, :] = (e1x - e1) - (e0y - e0)

    def update_row(s, x):
        for y, size in chunks:
            at, to, before = pl.ds(y, size), pl.ds(y + 8, size), pl.ds(y + 7, size)
            h, c = inv[x, at, :], coef[x, at, :]
            h0, h1, h2 = (curl[a, x + 1, to, :] for a in range(3))
            h0y, h2y = curl[0, x + 1, before, :], curl[2, x + 1, before, :]
            h1x, h2x = curl[1, x, to, :], curl[2, x, to, :]
            image = (
                (h2 - h2y) - h * (h1 - last_z(h1)),
                h * (h0 - last_z(h0)) - (h2 - h2x),
                (h1 - h1x) - (h0 - h0y),
            )
            shift = nz - 1 - (2 + s) * cells - x
            source = pltpu.roll(columns[at, :], shift, 1)
            source = jnp.where(lane_index(source.shape) == nz - 1, source, 0.0)
            for a in range(3):
                value = field[a, x, at, :] - c * image[a]
                field[a, x, at, :] = value + source if a == 2 else value

    def product_row(s, x):
        for y, size in chunks:
            at = pl.ds(y, size)
            value = sum(field[a, x, at, :] * terms[s, a, x, at, :].astype(jnp.float32) for a in range(3))
            total[x, at, :] = value if s == 0 else total[x, at, :] + value

    pl.semaphore_wait(barrier, 2)
    load_last.wait()
    send_high(0)
    load_rest.wait()
    send_low(0)

    def model_up():
        return pltpu.make_async_remote_copy(
            src_ref=model_ref.at[rows_v - 1],
            dst_ref=model_low,
            send_sem=model_send.at[0],
            recv_sem=model_recv.at[0],
            device_id=(grp, high),
            device_id_type=MESH,
        )

    def model_down():
        return pltpu.make_async_remote_copy(
            src_ref=model_ref.at[0],
            dst_ref=model_high,
            send_sem=model_send.at[1],
            recv_sem=model_recv.at[1],
            device_id=(grp, low),
            device_id_type=MESH,
        )

    @pl.when(has_high)
    def _():
        model_up().start()

    @pl.when(has_low)
    def _():
        model_down().start()

    load_coef.wait()

    def coefficient_row(x, carry):
        coef[x] = 0.05 * jnp.exp(-0.7 * coef[x])
        return carry

    lax.fori_loop(0, cells, coefficient_row, 0)

    @pl.when(jnp.logical_not(has_low))
    def _():
        model_low[...] = jnp.zeros_like(model_low)

    @pl.when(jnp.logical_not(has_high))
    def _():
        model_high[...] = jnp.zeros_like(model_high)
        for s in range(steps):
            from_high[s] = jnp.zeros(from_high.shape[1:], jnp.float32)

    def regularize():
        @pl.when(has_high)
        def _():
            model_up().wait_send()
            model_down().wait_recv()

        @pl.when(has_low)
        def _():
            model_down().wait_send()
            model_up().wait_recv()

        for v in range(rows_v):
            model[v, pl.ds(0, 8), :] = jnp.zeros((8, nz), jnp.float32)
            model[v, pl.ds(ny + 8, 8), :] = jnp.zeros((8, nz), jnp.float32)
            model[v, pl.ds(8, ny), :] = model_ref[v]
        for v in range(rows_v):
            for y, size in chunks:
                at = pl.ds(y, size)
                center = model_ref[v, at, :]
                below = model_low[at, :] if v == 0 else model_ref[v - 1, at, :]
                above = model_high[at, :] if v == rows_v - 1 else model_ref[v + 1, at, :]
                sides = model[v, pl.ds(y + 7, size), :] + model[v, pl.ds(y + 9, size), :]
                around = below + above + sides + next_z(center) + last_z(center)
                reg_ref[v, at, :] = 0.1 * (6.0 * center - around)

    def store(first, count, sem):
        return pltpu.make_async_copy(
            field.at[:, pl.ds(first, count), pl.ds(0, ny)], out_ref.at[:, pl.ds(first, count)], local_sem.at[sem]
        )

    for s in range(steps):

        def inner_curl(x, carry):
            curl_row(x, lambda at: (field[1, x + 1, at, :], field[2, x + 1, at, :]))
            return carry

        lax.fori_loop(0, cells - 1, inner_curl, 0)
        if s > 0:

            def late_product(x, carry):
                product_row(s - 1, x)
                return carry

            load_terms[s - 1].wait()
            lax.fori_loop(0, cells, late_product, 0)

        def inner_update(x, carry):
            update_row(s, x)
            return carry

        lax.fori_loop(1, cells - 1, inner_update, 0)
        if s == steps - 1:
            store(1, cells - 2, 3).start()
        if s == min(1, steps - 1):
            regularize()

        @pl.when(has_high)
        def _():
            copy_up(s).wait_send()
            copy_down(s).wait_recv()

        @pl.when(has_low)
        def _():
            copy_down(s).wait_send()
            copy_up(s).wait_recv()

        curl_row(cells - 1, lambda at: (from_high[s, 0, at, :], from_high[s, 1, at, :]))

        @pl.when(has_low)
        def _():
            for y, size in chunks:
                at, to = pl.ds(y, size), pl.ds(y + 8, size)
                curl[1, 0, to, :] = from_low[s, 0, at, :] - field[2, 0, at, :]
                curl[2, 0, to, :] = from_low[s, 1, at, :] + field[1, 0, at, :]

        @pl.when(jnp.logical_not(has_low))
        def _():
            for a in (1, 2):
                curl[a, 0] = jnp.zeros(curl.shape[2:], jnp.float32)

        update_row(s, cells - 1)
        if s < steps - 1:
            send_high(s + 1)
        update_row(s, 0)
        if s < steps - 1:
            send_low(s + 1)
    store(0, 1, 4).start()
    store(cells - 1, 1, 5).start()

    load_terms[steps - 1].wait()
    for x in range(cells):
        product_row(steps - 1, x)
        inside = lane_index((ny, nz)).astype(jnp.float32) < jnp.broadcast_to(
            columns[:, cells + x : cells + x + 1], (ny, nz)
        )
        sens_ref[x] = jnp.where(inside, -0.7 * coef[x] * total[x], 0.0)
    store(1, cells - 2, 3).wait()
    store(0, 1, 4).wait()
    store(cells - 1, 1, 5).wait()


def field_phase(n, adj, fwd, logc, spacing, residuals, gates, counts, model):
    steps = fwd.shape[0]
    cells, ny, nz = logc.shape
    f32 = jnp.float32
    anywhere, vmem = pl.BlockSpec(memory_space=pl.ANY), pl.BlockSpec(memory_space=pltpu.VMEM)
    dma = pltpu.SemaphoreType.DMA
    return pl.pallas_call(
        functools.partial(field_kernel, n),
        out_shape=(
            jax.ShapeDtypeStruct(adj.shape, f32),
            jax.ShapeDtypeStruct(logc.shape, f32),
            jax.ShapeDtypeStruct(model.shape, f32),
        ),
        in_specs=[anywhere] * 3 + [vmem, vmem, pl.BlockSpec(memory_space=pltpu.SMEM), vmem, vmem],
        out_specs=(anywhere, vmem, vmem),
        scratch_shapes=[
            pltpu.VMEM((3, cells, ny + 8, nz), f32),
            pltpu.VMEM((3, cells + 1, ny + 8, nz), f32),
            pltpu.VMEM((cells, ny, nz), f32),
            pltpu.VMEM((cells, ny, nz), f32),
            pltpu.VMEM((cells, ny, nz), f32),
            pltpu.VMEM(fwd.shape, jnp.bfloat16),
            pltpu.VMEM((ny, nz), f32),
            pltpu.VMEM((steps, 2, ny, nz), f32),
            pltpu.VMEM((steps, 2, ny, nz), f32),
            pltpu.VMEM((steps, 2, ny, nz), f32),
            pltpu.VMEM((model.shape[0], ny + 16, nz), f32),
            pltpu.VMEM((ny, nz), f32),
            pltpu.VMEM((ny, nz), f32),
            dma((6,)),
            dma((steps,)),
            dma((steps,)),
            dma((steps,)),
            dma((steps,)),
            dma((steps,)),
            dma((2,)),
            dma((2,)),
        ],
        compiler_params=pltpu.CompilerParams(collective_id=0, has_side_effects=True, vmem_limit_bytes=48 << 20),
    )(adj, fwd, logc, spacing, residuals, gates, counts, model)


def body(
    adjoint_in,
    forward_terms,
    log_conductivity,
    spacing,
    residuals,
    gate_index,
    counts,
    voxel_column,
    voxel_model,
):
    depth = adjoint_in.shape[3]
    tile_count = lax.axis_size("tx")
    adjoint, sensitivity, regularity = field_phase(
        tile_count,
        adjoint_in,
        forward_terms,
        log_conductivity,
        spacing,
        residuals,
        gate_index,
        counts,
        voxel_model,
    )
    column_count = counts.shape[0] * counts.shape[1]
    capacity = 2 * column_count // tile_count
    voxel_count = voxel_model.shape[0] * voxel_model.shape[1]
    columns = sensitivity.reshape(column_count, depth)
    voxel_ids = voxel_column.reshape(column_count)
    target = voxel_ids // voxel_count
    local_voxel = voxel_ids % voxel_count
    one_hot = (target[:, None] == jnp.arange(tile_count, dtype=jnp.int32)[None, :]).astype(
        jnp.int32
    )
    slot_rank = jnp.sum((jnp.cumsum(one_hot, axis=0) - 1) * one_hot, axis=1)
    position = target * capacity + slot_rank
    send_rows = jnp.zeros((tile_count * capacity, depth), jnp.float32).at[position].set(columns)
    send_ids = jnp.full((tile_count * capacity,), -1, jnp.int32).at[position].set(local_voxel)
    received, received_ids = (
        lax.all_to_all(
            send_rows.reshape(tile_count, capacity, depth),
            "tx",
            split_axis=0,
            concat_axis=0,
            tiled=True,
        ),
        lax.all_to_all(
            send_ids.reshape(tile_count, capacity), "tx", split_axis=0, concat_axis=0, tiled=True
        ),
    )
    received = received.reshape(tile_count * capacity, depth)
    received_ids = received_ids.reshape(tile_count * capacity)
    selector = (jnp.arange(voxel_count, dtype=jnp.int32)[:, None] == received_ids[None, :]).astype(
        jnp.float32
    )
    collected = jnp.dot(
        selector, received, precision=lax.Precision.HIGHEST, preferred_element_type=jnp.float32
    )
    collected = collected.reshape(voxel_model.shape)
    return (adjoint, collected + regularity)


def solution(mesh):
    in_specs = (
        P(None, ("grp", "tx"), None, None),
        P(None, None, ("grp", "tx"), None, None),
        P(("grp", "tx"), None, None),
        P(("grp", "tx"), None),
        P(None, ("grp", "tx"), None),
        P("grp"),
        P(("grp", "tx"), None),
        P(("grp", "tx"), None),
        P(("grp", "tx"), None, None),
    )
    out_specs = (P(None, ("grp", "tx"), None, None), P(("grp", "tx"), None, None))
    return jax.shard_map(body, mesh=mesh, in_specs=in_specs, out_specs=out_specs, check_vma=False)
```

```python
import functools

import jax
import jax.numpy as jnp
from jax import lax
from jax.experimental import pallas as pl
from jax.experimental.pallas import tpu as pltpu
from jax.sharding import PartitionSpec as P

MESH = pl.DeviceIdType.MESH


def lane_index(shape):
    return lax.broadcasted_iota(jnp.int32, shape, 1)


def next_z(value):
    depth = value.shape[1]
    return jnp.where(lane_index(value.shape) < depth - 1, pltpu.roll(value, depth - 1, 1), 0.0)


def last_z(value):
    return jnp.where(lane_index(value.shape) > 0, pltpu.roll(value, 1, 1), 0.0)


def field_kernel(
    n,
    adj_ref,
    fwd_ref,
    logc_ref,
    spacing_hbm,
    residual_hbm,
    gate_ref,
    counts_hbm,
    model_hbm,
    out_ref,
    sens_ref,
    reg_ref,
    spacing_ref,
    residual_ref,
    counts_ref,
    model_ref,
    field,
    curl,
    coef,
    inv,
    total,
    terms,
    columns,
    from_low,
    from_high,
    to_high,
    model,
    model_low,
    model_high,
    local_sem,
    term_sem,
    send_up,
    send_down,
    recv_low,
    recv_high,
    model_send,
    model_recv,
):
    steps = fwd_ref.shape[0]
    cells, ny, nz = logc_ref.shape
    rows_v = model_hbm.shape[0]
    grp, me = lax.axis_index("grp"), lax.axis_index("tx")
    low, high = lax.rem(me + n - 1, n), lax.rem(me + 1, n)
    has_low, has_high = me > 0, me < n - 1
    chunk = 64
    chunks = [(y, chunk) for y in range(0, ny, chunk)]

    small = [
        pltpu.make_async_copy(source, target, local_sem.at[6 + i])
        for i, (source, target) in enumerate(
            (
                (spacing_hbm, spacing_ref),
                (counts_hbm, counts_ref),
                (residual_hbm, residual_ref),
                (model_hbm, model_ref),
            )
        )
    ]
    for copy in small[:3]:
        copy.start()
    load_last = pltpu.make_async_copy(
        adj_ref.at[:, pl.ds(cells - 1, 1)], field.at[:, pl.ds(cells - 1, 1), pl.ds(0, ny)], local_sem.at[0]
    )
    load_last.start()
    load_rest = pltpu.make_async_copy(
        adj_ref.at[:, pl.ds(0, cells - 1)], field.at[:, pl.ds(0, cells - 1), pl.ds(0, ny)], local_sem.at[1]
    )
    load_rest.start()
    load_coef = pltpu.make_async_copy(logc_ref, coef, local_sem.at[2])
    load_coef.start()
    load_terms = [pltpu.make_async_copy(fwd_ref.at[s], terms.at[s], term_sem.at[s]) for s in range(steps)]
    for copy in load_terms:
        copy.start()
    small[3].start()

    barrier = pltpu.get_barrier_semaphore()
    for neighbour in (low, high):
        pl.semaphore_signal(barrier, inc=1, device_id=(grp, neighbour), device_id_type=MESH)

    for copy in small[:3]:
        copy.wait()
    inverse = 1.0 / spacing_ref[...]
    depth_count = counts_ref[...].astype(jnp.float32)
    sources = [residual_ref[gate_ref[s]] for s in range(steps)]
    for y in range(0, ny, nz):
        parts = [v[:, y : y + nz] for v in [inverse, depth_count] + sources]
        parts.append(jnp.zeros((nz - cells * (2 + steps), nz), jnp.float32))
        columns[pl.ds(y, nz), :] = jnp.concatenate(parts, axis=0).T

    for x in range(cells):
        inv[x] = jnp.broadcast_to(columns[:, x : x + 1], (ny, nz))
        for a in range(3):
            field[a, x, pl.ds(ny, 8), :] = jnp.zeros((8, nz), jnp.float32)
            curl[a, x + 1, pl.ds(0, 8), :] = jnp.zeros((8, nz), jnp.float32)

    def copy_up(slot):
        return pltpu.make_async_remote_copy(
            src_ref=to_high.at[slot],
            dst_ref=from_low.at[slot],
            send_sem=send_up.at[slot],
            recv_sem=recv_low.at[slot],
            device_id=(grp, high),
            device_id_type=MESH,
        )

    def copy_down(slot):
        return pltpu.make_async_remote_copy(
            src_ref=field.at[pl.ds(1, 2), 0, pl.ds(0, ny)],
            dst_ref=from_high.at[slot],
            send_sem=send_down.at[slot],
            recv_sem=recv_high.at[slot],
            device_id=(grp, low),
            device_id_type=MESH,
        )

    def send_high(slot):
        x = cells - 1
        for y, size in chunks:
            e0, e1, e2 = (field[a, x, pl.ds(y, size), :] for a in range(3))
            e0y = field[0, x, pl.ds(y + 1, size), :]
            to_high[slot, 0, pl.ds(y, size), :] = inv[x, pl.ds(y, size), :] * (next_z(e0) - e0) + e2
            to_high[slot, 1, pl.ds(y, size), :] = (e0 - e0y) - e1

        @pl.when(has_high)
        def _():
            copy_up(slot).start()

    def send_low(slot):
        @pl.when(has_low)
        def _():
            copy_down(slot).start()

    def curl_row(x, next_row):
        for y, size in chunks:
            at = pl.ds(y, size)
            e0, e1, e2 = (field[a, x, at, :] for a in range(3))
            e0y, e2y = field[0, x, pl.ds(y + 1, size), :], field[2, x, pl.ds(y + 1, size), :]
            e1x, e2x = next_row(at)
            h = inv[x, at, :]
            to = pl.ds(y + 8, size)
            curl[0, x + 1, to, :] = (e2y - e2) - h * (next_z(e1) - e1)
            curl[1, x + 1, to, :] = h * (next_z(e0) - e0) - (e2x - e2)
            curl[2, x + 1, to, :] = (e1x - e1) - (e0y - e0)

    def update_row(s, x):
        for y, size in chunks:
            at, to, before = pl.ds(y, size), pl.ds(y + 8, size), pl.ds(y + 7, size)
            h, c = inv[x, at, :], coef[x, at, :]
            h0, h1, h2 = (curl[a, x + 1, to, :] for a in range(3))
            h0y, h2y = curl[0, x + 1, before, :], curl[2, x + 1, before, :]
            h1x, h2x = curl[1, x, to, :], curl[2, x, to, :]
            image = (
                (h2 - h2y) - h * (h1 - last_z(h1)),
                h * (h0 - last_z(h0)) - (h2 - h2x),
                (h1 - h1x) - (h0 - h0y),
            )
            shift = nz - 1 - (2 + s) * cells - x
            source = pltpu.roll(columns[at, :], shift, 1)
            source = jnp.where(lane_index(source.shape) == nz - 1, source, 0.0)
            for a in range(3):
                value = field[a, x, at, :] - c * image[a]
                field[a, x, at, :] = value + source if a == 2 else value

    def product_row(s, x):
        for y, size in chunks:
            at = pl.ds(y, size)
            value = sum(field[a, x, at, :] * terms[s, a, x, at, :].astype(jnp.float32) for a in range(3))
            total[x, at, :] = value if s == 0 else total[x, at, :] + value

    pl.semaphore_wait(barrier, 2)
    load_last.wait()
    send_high(0)
    load_rest.wait()
    send_low(0)

    def model_up():
        return pltpu.make_async_remote_copy(
            src_ref=model_hbm.at[rows_v - 1],
            dst_ref=model_low,
            send_sem=model_send.at[0],
            recv_sem=model_recv.at[0],
            device_id=(grp, high),
            device_id_type=MESH,
        )

    def model_down():
        return pltpu.make_async_remote_copy(
            src_ref=model_hbm.at[0],
            dst_ref=model_high,
            send_sem=model_send.at[1],
            recv_sem=model_recv.at[1],
            device_id=(grp, low),
            device_id_type=MESH,
        )

    @pl.when(has_high)
    def _():
        model_up().start()

    @pl.when(has_low)
    def _():
        model_down().start()

    load_coef.wait()

    def coefficient_row(x, carry):
        coef[x] = 0.05 * jnp.exp(-0.7 * coef[x])
        return carry

    lax.fori_loop(0, cells, coefficient_row, 0)

    @pl.when(jnp.logical_not(has_low))
    def _():
        model_low[...] = jnp.zeros_like(model_low)

    @pl.when(jnp.logical_not(has_high))
    def _():
        model_high[...] = jnp.zeros_like(model_high)
        for s in range(steps):
            from_high[s] = jnp.zeros(from_high.shape[1:], jnp.float32)

    def regularize():
        @pl.when(has_high)
        def _():
            model_up().wait_send()
            model_down().wait_recv()

        @pl.when(has_low)
        def _():
            model_down().wait_send()
            model_up().wait_recv()

        small[3].wait()
        for v in range(rows_v):
            model[v, pl.ds(0, 8), :] = jnp.zeros((8, nz), jnp.float32)
            model[v, pl.ds(ny + 8, 8), :] = jnp.zeros((8, nz), jnp.float32)
            model[v, pl.ds(8, ny), :] = model_ref[v]
        for v in range(rows_v):
            for y, size in chunks:
                at = pl.ds(y, size)
                center = model_ref[v, at, :]
                below = model_low[at, :] if v == 0 else model_ref[v - 1, at, :]
                above = model_high[at, :] if v == rows_v - 1 else model_ref[v + 1, at, :]
                sides = model[v, pl.ds(y + 7, size), :] + model[v, pl.ds(y + 9, size), :]
                around = below + above + sides + next_z(center) + last_z(center)
                reg_ref[v, at, :] = 0.1 * (6.0 * center - around)

    def store(first, count, sem):
        return pltpu.make_async_copy(
            field.at[:, pl.ds(first, count), pl.ds(0, ny)], out_ref.at[:, pl.ds(first, count)], local_sem.at[sem]
        )

    for s in range(steps):

        def inner_curl(x, carry):
            curl_row(x, lambda at: (field[1, x + 1, at, :], field[2, x + 1, at, :]))
            return carry

        lax.fori_loop(0, cells - 1, inner_curl, 0)
        if s > 0:

            def late_product(x, carry):
                product_row(s - 1, x)
                return carry

            load_terms[s - 1].wait()
            lax.fori_loop(0, cells, late_product, 0)

        def inner_update(x, carry):
            update_row(s, x)
            return carry

        lax.fori_loop(1, cells - 1, inner_update, 0)
        if s == steps - 1:
            store(1, cells - 2, 3).start()
        if s == min(1, steps - 1):
            regularize()

        @pl.when(has_high)
        def _():
            copy_up(s).wait_send()
            copy_down(s).wait_recv()

        @pl.when(has_low)
        def _():
            copy_down(s).wait_send()
            copy_up(s).wait_recv()

        curl_row(cells - 1, lambda at: (from_high[s, 0, at, :], from_high[s, 1, at, :]))

        @pl.when(has_low)
        def _():
            for y, size in chunks:
                at, to = pl.ds(y, size), pl.ds(y + 8, size)
                curl[1, 0, to, :] = from_low[s, 0, at, :] - field[2, 0, at, :]
                curl[2, 0, to, :] = from_low[s, 1, at, :] + field[1, 0, at, :]

        @pl.when(jnp.logical_not(has_low))
        def _():
            for a in (1, 2):
                curl[a, 0] = jnp.zeros(curl.shape[2:], jnp.float32)

        update_row(s, cells - 1)
        if s < steps - 1:
            send_high(s + 1)
        update_row(s, 0)
        if s < steps - 1:
            send_low(s + 1)
    store(0, 1, 4).start()
    store(cells - 1, 1, 5).start()

    load_terms[steps - 1].wait()
    for x in range(cells):
        product_row(steps - 1, x)
        inside = lane_index((ny, nz)).astype(jnp.float32) < jnp.broadcast_to(
            columns[:, cells + x : cells + x + 1], (ny, nz)
        )
        sens = jnp.where(inside, -0.7 * coef[x] * total[x], 0.0)
        coarse = sens.astype(jnp.bfloat16)
        sens_ref[x, :, 0:nz] = coarse
        sens_ref[x, :, nz : 2 * nz] = (sens - coarse.astype(jnp.float32)).astype(jnp.bfloat16)
    store(1, cells - 2, 3).wait()
    store(0, 1, 4).wait()
    store(cells - 1, 1, 5).wait()


def field_phase(n, adj, fwd, logc, spacing, residuals, gates, counts, model):
    steps = fwd.shape[0]
    cells, ny, nz = logc.shape
    f32 = jnp.float32
    anywhere, vmem = pl.BlockSpec(memory_space=pl.ANY), pl.BlockSpec(memory_space=pltpu.VMEM)
    dma = pltpu.SemaphoreType.DMA
    return pl.pallas_call(
        functools.partial(field_kernel, n),
        out_shape=(
            jax.ShapeDtypeStruct(adj.shape, f32),
            jax.ShapeDtypeStruct((cells, ny, 2 * nz), jnp.bfloat16),
            jax.ShapeDtypeStruct(model.shape, f32),
        ),
        in_specs=[anywhere] * 5 + [pl.BlockSpec(memory_space=pltpu.SMEM), anywhere, anywhere],
        out_specs=(anywhere, vmem, vmem),
        scratch_shapes=[
            pltpu.VMEM(spacing.shape, f32),
            pltpu.VMEM(residuals.shape, f32),
            pltpu.VMEM(counts.shape, jnp.int32),
            pltpu.VMEM(model.shape, f32),
            pltpu.VMEM((3, cells, ny + 8, nz), f32),
            pltpu.VMEM((3, cells + 1, ny + 8, nz), f32),
            pltpu.VMEM((cells, ny, nz), f32),
            pltpu.VMEM((cells, ny, nz), f32),
            pltpu.VMEM((cells, ny, nz), f32),
            pltpu.VMEM(fwd.shape, jnp.bfloat16),
            pltpu.VMEM((ny, nz), f32),
            pltpu.VMEM((steps, 2, ny, nz), f32),
            pltpu.VMEM((steps, 2, ny, nz), f32),
            pltpu.VMEM((steps, 2, ny, nz), f32),
            pltpu.VMEM((model.shape[0], ny + 16, nz), f32),
            pltpu.VMEM((ny, nz), f32),
            pltpu.VMEM((ny, nz), f32),
            dma((10,)),
            dma((steps,)),
            dma((steps,)),
            dma((steps,)),
            dma((steps,)),
            dma((steps,)),
            dma((2,)),
            dma((2,)),
        ],
        compiler_params=pltpu.CompilerParams(collective_id=0, has_side_effects=True, vmem_limit_bytes=48 << 20),
    )(adj, fwd, logc, spacing, residuals, gates, counts, model)


def relayout_kernel(
    n,
    sens_hbm,
    voxel_hbm,
    reg_hbm,
    out_ref,
    sens,
    voxel,
    ids,
    reg,
    to_pair,
    from_pair,
    across,
    from_across,
    held,
    arrived,
    load_sem,
    pair_send,
    pair_recv,
    across_send,
    across_recv,
    layer_send,
    layer_recv,
):
    layers = n // 4
    cells, ny = voxel_hbm.shape
    voxels, nz = reg_hbm.shape
    grp, me = lax.axis_index("grp"), lax.axis_index("tx")
    core, half, layer = lax.rem(me, 2), lax.rem(me // 2, 2), me // 4
    up = jnp.where(layer < layers // 2, 1, 0)

    def tile(z, y, c):
        return (z * 2 + y) * 2 + c

    def layer_at(k):
        return up * (layers - 1 - k) + (1 - up) * k

    loads = [
        pltpu.make_async_copy(source, target, load_sem.at[i])
        for i, (source, target) in enumerate(((sens_hbm, sens), (voxel_hbm, voxel), (reg_hbm, reg)))
    ]
    for copy in loads:
        copy.start()
    barrier = pltpu.get_barrier_semaphore()
    for other in (tile(layer, half, 1 - core), tile(layer, 1 - half, core)):
        pl.semaphore_signal(barrier, inc=1, device_id=(grp, other), device_id_type=MESH)

    def greet(z, carry):
        @pl.when(z != layer)
        def _():
            pl.semaphore_signal(
                barrier, inc=1, device_id=(grp, tile(z, half, core)), device_id_type=MESH
            )

        return carry

    lax.fori_loop(0, layers, greet, 0)
    for copy in loads:
        copy.wait()
    for x in range(cells):
        ids[:, x * ny : (x + 1) * ny] = voxel[x : x + 1, :]

    def pair_copy(k, y):
        return pltpu.make_async_remote_copy(
            src_ref=to_pair.at[k, y],
            dst_ref=from_pair.at[k, y],
            send_sem=pair_send.at[k, y],
            recv_sem=pair_recv.at[k, y],
            device_id=(grp, tile(layer, half, 1 - core)),
            device_id_type=MESH,
        )

    def across_copy(k):
        return pltpu.make_async_remote_copy(
            src_ref=across.at[k],
            dst_ref=from_across.at[k],
            send_sem=across_send.at[k],
            recv_sem=across_recv.at[k],
            device_id=(grp, tile(layer, 1 - half, core)),
            device_id_type=MESH,
        )

    def layer_copy(k):
        return pltpu.make_async_remote_copy(
            src_ref=held.at[k],
            dst_ref=arrived.at[layer],
            send_sem=layer_send.at[k],
            recv_sem=layer_recv.at[layer],
            device_id=(grp, tile(layer_at(k), half, core)),
            device_id_type=MESH,
        )

    def arrival(z):
        return pltpu.make_async_remote_copy(
            src_ref=held.at[0],
            dst_ref=arrived.at[z],
            send_sem=layer_send.at[0],
            recv_sem=layer_recv.at[z],
            device_id=(grp, tile(z, half, core)),
            device_id_type=MESH,
        )

    size = 256

    def partial_sums(target, put):
        for first in range(0, voxels, size):
            wanted = lax.broadcasted_iota(jnp.int32, (size, cells * ny), 0)
            here = wanted == ids[...] - (target * voxels + first)
            picked = jnp.where(here, 1.0, 0.0).astype(jnp.bfloat16)
            sums = jnp.dot(picked, sens[...], preferred_element_type=jnp.float32)
            put(pl.ds(first, size), sums[:, 0:nz] + sums[:, nz : 2 * nz])

    def forward(k):
        across_copy(k).wait_recv()
        pair_copy(k, 1).wait_recv()
        held[k] = held[k] + from_pair[k, 1] + from_across[k]

        @pl.when(layer_at(k) != layer)
        def _():
            layer_copy(k).start()

    def stage(k, carry):
        z = layer_at(k)

        def put_pair(y):
            def put(at, value):
                to_pair[k, y, at, :] = value

            return put

        def put_across(at, value):
            across[k, at, :] = value

        def put_held(at, value):
            held[k, at, :] = value

        partial_sums(tile(z, 1 - half, 1 - core), put_pair(0))

        @pl.when(k == 0)
        def _():
            pl.semaphore_wait(barrier, layers + 1)

        pair_copy(k, 0).start()
        partial_sums(tile(z, 1 - half, core), put_across)
        pair_copy(k, 0).wait_recv()
        across[k] = across[k] + from_pair[k, 0]
        across_copy(k).start()
        partial_sums(tile(z, half, 1 - core), put_pair(1))
        pair_copy(k, 1).start()
        partial_sums(tile(z, half, core), put_held)

        @pl.when(k > 0)
        def _():
            forward(k - 1)

        return carry

    lax.fori_loop(0, layers, stage, 0)
    forward(layers - 1)
    own = up * (layers - 1 - layer) + (1 - up) * layer
    out_ref[...] = reg[...] + held[own]

    def collect(z, carry):
        @pl.when(z != layer)
        def _():
            arrival(z).wait_recv()
            out_ref[...] = out_ref[...] + arrived[z]

        return carry

    lax.fori_loop(0, layers, collect, 0)

    def drain(k, carry):
        pair_copy(k, 0).wait_send()
        pair_copy(k, 1).wait_send()
        across_copy(k).wait_send()

        @pl.when(layer_at(k) != layer)
        def _():
            layer_copy(k).wait_send()

        return carry

    lax.fori_loop(0, layers, drain, 0)


def relayout(n, sensitivity, voxel_column, regularity):
    cells, ny = voxel_column.shape
    nz = regularity.shape[2]
    voxels = regularity.shape[0] * regularity.shape[1]
    layers = n // 4
    f32, dma = jnp.float32, pltpu.SemaphoreType.DMA
    anywhere = pl.BlockSpec(memory_space=pl.ANY)
    block = (voxels, nz)
    out = pl.pallas_call(
        functools.partial(relayout_kernel, n),
        out_shape=jax.ShapeDtypeStruct(block, f32),
        in_specs=[anywhere] * 3,
        out_specs=pl.BlockSpec(memory_space=pltpu.VMEM),
        scratch_shapes=[
            pltpu.VMEM((cells * ny, 2 * nz), jnp.bfloat16),
            pltpu.VMEM((cells, ny), jnp.int32),
            pltpu.VMEM((1, cells * ny), jnp.int32),
            pltpu.VMEM(block, f32),
            pltpu.VMEM((layers, 2) + block, f32),
            pltpu.VMEM((layers, 2) + block, f32),
            pltpu.VMEM((layers,) + block, f32),
            pltpu.VMEM((layers,) + block, f32),
            pltpu.VMEM((layers,) + block, f32),
            pltpu.VMEM((layers,) + block, f32),
            dma((3,)),
            dma((layers, 2)),
            dma((layers, 2)),
            dma((layers,)),
            dma((layers,)),
            dma((layers,)),
            dma((layers,)),
        ],
        compiler_params=pltpu.CompilerParams(collective_id=1, has_side_effects=True, vmem_limit_bytes=52 << 20),
    )(sensitivity.reshape(cells * ny, 2 * nz), voxel_column, regularity.reshape(block))
    return out.reshape(regularity.shape)


def body(
    adjoint_in,
    forward_terms,
    log_conductivity,
    spacing,
    residuals,
    gate_index,
    counts,
    voxel_column,
    voxel_model,
):
    tile_count = lax.axis_size("tx")
    adjoint, sensitivity, regularity = field_phase(
        tile_count,
        adjoint_in,
        forward_terms,
        log_conductivity,
        spacing,
        residuals,
        gate_index,
        counts,
        voxel_model,
    )
    gradient = relayout(tile_count, sensitivity, voxel_column, regularity)
    return (adjoint, gradient)


def solution(mesh):
    in_specs = (
        P(None, ("grp", "tx"), None, None),
        P(None, None, ("grp", "tx"), None, None),
        P(("grp", "tx"), None, None),
        P(("grp", "tx"), None),
        P(None, ("grp", "tx"), None),
        P("grp"),
        P(("grp", "tx"), None),
        P(("grp", "tx"), None),
        P(("grp", "tx"), None, None),
    )
    out_specs = (P(None, ("grp", "tx"), None, None), P(("grp", "tx"), None, None))
    return jax.shard_map(body, mesh=mesh, in_specs=in_specs, out_specs=out_specs, check_vma=False)
```

```python
import functools

import jax
import jax.numpy as jnp
from jax import lax
from jax.experimental import pallas as pl
from jax.experimental.pallas import tpu as pltpu
from jax.sharding import PartitionSpec as P

MESH = pl.DeviceIdType.MESH


def lane_index(shape):
    return lax.broadcasted_iota(jnp.int32, shape, 1)


def next_z(value):
    depth = value.shape[1]
    return jnp.where(lane_index(value.shape) < depth - 1, pltpu.roll(value, depth - 1, 1), 0.0)


def last_z(value):
    return jnp.where(lane_index(value.shape) > 0, pltpu.roll(value, 1, 1), 0.0)


def field_kernel(
    n,
    adj_ref,
    fwd_ref,
    logc_ref,
    spacing_hbm,
    residual_hbm,
    gate_ref,
    counts_hbm,
    model_hbm,
    out_ref,
    sens_ref,
    reg_ref,
    spacing_ref,
    residual_ref,
    counts_ref,
    model_ref,
    field,
    curl,
    coef,
    inv,
    total,
    terms,
    columns,
    from_low,
    from_high,
    to_high,
    model,
    model_low,
    model_high,
    local_sem,
    term_sem,
    send_up,
    send_down,
    recv_low,
    recv_high,
    model_send,
    model_recv,
):
    steps = fwd_ref.shape[0]
    cells, ny, nz = logc_ref.shape
    rows_v = model_hbm.shape[0]
    grp, me = lax.axis_index("grp"), lax.axis_index("tx")
    low, high = lax.rem(me + n - 1, n), lax.rem(me + 1, n)
    has_low, has_high = me > 0, me < n - 1
    chunk = 64
    chunks = [(y, chunk) for y in range(0, ny, chunk)]

    small = [
        pltpu.make_async_copy(source, target, local_sem.at[6 + i])
        for i, (source, target) in enumerate(
            (
                (spacing_hbm, spacing_ref),
                (counts_hbm, counts_ref),
                (residual_hbm, residual_ref),
                (model_hbm, model_ref),
            )
        )
    ]
    for copy in small[:3]:
        copy.start()
    load_last = pltpu.make_async_copy(
        adj_ref.at[:, pl.ds(cells - 1, 1)], field.at[:, pl.ds(cells - 1, 1), pl.ds(0, ny)], local_sem.at[0]
    )
    load_last.start()
    load_rest = pltpu.make_async_copy(
        adj_ref.at[:, pl.ds(0, cells - 1)], field.at[:, pl.ds(0, cells - 1), pl.ds(0, ny)], local_sem.at[1]
    )
    load_rest.start()
    load_coef = pltpu.make_async_copy(logc_ref, coef, local_sem.at[2])
    load_coef.start()
    load_terms = [pltpu.make_async_copy(fwd_ref.at[s], terms.at[s], term_sem.at[s]) for s in range(steps)]
    for copy in load_terms:
        copy.start()
    small[3].start()

    barrier = pltpu.get_barrier_semaphore()
    for neighbour in (low, high):
        pl.semaphore_signal(barrier, inc=1, device_id=(grp, neighbour), device_id_type=MESH)

    for copy in small[:3]:
        copy.wait()
    inverse = 1.0 / spacing_ref[...]
    depth_count = counts_ref[...].astype(jnp.float32)
    sources = [residual_ref[gate_ref[s]] for s in range(steps)]
    for y in range(0, ny, nz):
        parts = [v[:, y : y + nz] for v in [inverse, depth_count] + sources]
        parts.append(jnp.zeros((nz - cells * (2 + steps), nz), jnp.float32))
        columns[pl.ds(y, nz), :] = jnp.concatenate(parts, axis=0).T

    for x in range(cells):
        inv[x] = jnp.broadcast_to(columns[:, x : x + 1], (ny, nz))
        for a in range(3):
            field[a, x, pl.ds(ny, 8), :] = jnp.zeros((8, nz), jnp.float32)
            curl[a, x + 1, pl.ds(0, 8), :] = jnp.zeros((8, nz), jnp.float32)

    def copy_up(slot):
        return pltpu.make_async_remote_copy(
            src_ref=to_high.at[slot],
            dst_ref=from_low.at[slot],
            send_sem=send_up.at[slot],
            recv_sem=recv_low.at[slot],
            device_id=(grp, high),
            device_id_type=MESH,
        )

    def copy_down(slot):
        return pltpu.make_async_remote_copy(
            src_ref=field.at[pl.ds(1, 2), 0, pl.ds(0, ny)],
            dst_ref=from_high.at[slot],
            send_sem=send_down.at[slot],
            recv_sem=recv_high.at[slot],
            device_id=(grp, low),
            device_id_type=MESH,
        )

    def send_high(slot):
        x = cells - 1
        for y, size in chunks:
            e0, e1, e2 = (field[a, x, pl.ds(y, size), :] for a in range(3))
            e0y = field[0, x, pl.ds(y + 1, size), :]
            to_high[slot, 0, pl.ds(y, size), :] = inv[x, pl.ds(y, size), :] * (next_z(e0) - e0) + e2
            to_high[slot, 1, pl.ds(y, size), :] = (e0 - e0y) - e1

        @pl.when(has_high)
        def _():
            copy_up(slot).start()

    def send_low(slot):
        @pl.when(has_low)
        def _():
            copy_down(slot).start()

    def curl_row(x, next_row):
        for y, size in chunks:
            at = pl.ds(y, size)
            e0, e1, e2 = (field[a, x, at, :] for a in range(3))
            e0y, e2y = field[0, x, pl.ds(y + 1, size), :], field[2, x, pl.ds(y + 1, size), :]
            e1x, e2x = next_row(at)
            h = inv[x, at, :]
            to = pl.ds(y + 8, size)
            curl[0, x + 1, to, :] = (e2y - e2) - h * (next_z(e1) - e1)
            curl[1, x + 1, to, :] = h * (next_z(e0) - e0) - (e2x - e2)
            curl[2, x + 1, to, :] = (e1x - e1) - (e0y - e0)

    def update_row(s, x):
        for y, size in chunks:
            at, to, before = pl.ds(y, size), pl.ds(y + 8, size), pl.ds(y + 7, size)
            h, c = inv[x, at, :], coef[x, at, :]
            h0, h1, h2 = (curl[a, x + 1, to, :] for a in range(3))
            h0y, h2y = curl[0, x + 1, before, :], curl[2, x + 1, before, :]
            h1x, h2x = curl[1, x, to, :], curl[2, x, to, :]
            image = (
                (h2 - h2y) - h * (h1 - last_z(h1)),
                h * (h0 - last_z(h0)) - (h2 - h2x),
                (h1 - h1x) - (h0 - h0y),
            )
            shift = nz - 1 - (2 + s) * cells - x
            source = pltpu.roll(columns[at, :], shift, 1)
            source = jnp.where(lane_index(source.shape) == nz - 1, source, 0.0)
            for a in range(3):
                value = field[a, x, at, :] - c * image[a]
                field[a, x, at, :] = value + source if a == 2 else value

    def product_row(s, x):
        for y, size in chunks:
            at = pl.ds(y, size)
            value = sum(field[a, x, at, :] * terms[s, a, x, at, :].astype(jnp.float32) for a in range(3))
            total[x, at, :] = value if s == 0 else total[x, at, :] + value

    pl.semaphore_wait(barrier, 2)
    load_last.wait()
    send_high(0)
    load_rest.wait()
    send_low(0)

    def model_up():
        return pltpu.make_async_remote_copy(
            src_ref=model_hbm.at[rows_v - 1],
            dst_ref=model_low,
            send_sem=model_send.at[0],
            recv_sem=model_recv.at[0],
            device_id=(grp, high),
            device_id_type=MESH,
        )

    def model_down():
        return pltpu.make_async_remote_copy(
            src_ref=model_hbm.at[0],
            dst_ref=model_high,
            send_sem=model_send.at[1],
            recv_sem=model_recv.at[1],
            device_id=(grp, low),
            device_id_type=MESH,
        )

    @pl.when(has_high)
    def _():
        model_up().start()

    @pl.when(has_low)
    def _():
        model_down().start()

    load_coef.wait()

    def coefficient_row(x, carry):
        coef[x] = 0.05 * jnp.exp(-0.7 * coef[x])
        return carry

    lax.fori_loop(0, cells, coefficient_row, 0)

    @pl.when(jnp.logical_not(has_low))
    def _():
        model_low[...] = jnp.zeros_like(model_low)

    @pl.when(jnp.logical_not(has_high))
    def _():
        model_high[...] = jnp.zeros_like(model_high)
        for s in range(steps):
            from_high[s] = jnp.zeros(from_high.shape[1:], jnp.float32)

    def regularize():
        @pl.when(has_high)
        def _():
            model_up().wait_send()
            model_down().wait_recv()

        @pl.when(has_low)
        def _():
            model_down().wait_send()
            model_up().wait_recv()

        small[3].wait()
        for v in range(rows_v):
            model[v, pl.ds(0, 8), :] = jnp.zeros((8, nz), jnp.float32)
            model[v, pl.ds(ny + 8, 8), :] = jnp.zeros((8, nz), jnp.float32)
            model[v, pl.ds(8, ny), :] = model_ref[v]
        for v in range(rows_v):
            for y, size in chunks:
                at = pl.ds(y, size)
                center = model_ref[v, at, :]
                below = model_low[at, :] if v == 0 else model_ref[v - 1, at, :]
                above = model_high[at, :] if v == rows_v - 1 else model_ref[v + 1, at, :]
                sides = model[v, pl.ds(y + 7, size), :] + model[v, pl.ds(y + 9, size), :]
                around = below + above + sides + next_z(center) + last_z(center)
                reg_ref[v, at, :] = 0.1 * (6.0 * center - around)

    def store(first, count, sem):
        return pltpu.make_async_copy(
            field.at[:, pl.ds(first, count), pl.ds(0, ny)], out_ref.at[:, pl.ds(first, count)], local_sem.at[sem]
        )

    for s in range(steps):

        def inner_curl(x, carry):
            curl_row(x, lambda at: (field[1, x + 1, at, :], field[2, x + 1, at, :]))
            return carry

        lax.fori_loop(0, cells - 1, inner_curl, 0)
        if s > 0:

            def late_product(x, carry):
                product_row(s - 1, x)
                return carry

            load_terms[s - 1].wait()
            lax.fori_loop(0, cells, late_product, 0)

        def inner_update(x, carry):
            update_row(s, x)
            return carry

        lax.fori_loop(1, cells - 1, inner_update, 0)
        if s == steps - 1:
            store(1, cells - 2, 3).start()
        if s == min(1, steps - 1):
            regularize()

        @pl.when(has_high)
        def _():
            copy_up(s).wait_send()
            copy_down(s).wait_recv()

        @pl.when(has_low)
        def _():
            copy_down(s).wait_send()
            copy_up(s).wait_recv()

        curl_row(cells - 1, lambda at: (from_high[s, 0, at, :], from_high[s, 1, at, :]))

        @pl.when(has_low)
        def _():
            for y, size in chunks:
                at, to = pl.ds(y, size), pl.ds(y + 8, size)
                curl[1, 0, to, :] = from_low[s, 0, at, :] - field[2, 0, at, :]
                curl[2, 0, to, :] = from_low[s, 1, at, :] + field[1, 0, at, :]

        @pl.when(jnp.logical_not(has_low))
        def _():
            for a in (1, 2):
                curl[a, 0] = jnp.zeros(curl.shape[2:], jnp.float32)

        update_row(s, cells - 1)
        if s < steps - 1:
            send_high(s + 1)
        update_row(s, 0)
        if s < steps - 1:
            send_low(s + 1)
    store(0, 1, 4).start()
    store(cells - 1, 1, 5).start()

    load_terms[steps - 1].wait()
    for x in range(cells):
        product_row(steps - 1, x)
        inside = lane_index((ny, nz)).astype(jnp.float32) < jnp.broadcast_to(
            columns[:, cells + x : cells + x + 1], (ny, nz)
        )
        sens = jnp.where(inside, -0.7 * coef[x] * total[x], 0.0)
        coarse = sens.astype(jnp.bfloat16)
        sens_ref[x, :, 0:nz] = coarse
        sens_ref[x, :, nz : 2 * nz] = (sens - coarse.astype(jnp.float32)).astype(jnp.bfloat16)
    store(1, cells - 2, 3).wait()
    store(0, 1, 4).wait()
    store(cells - 1, 1, 5).wait()


def field_phase(n, adj, fwd, logc, spacing, residuals, gates, counts, model):
    steps = fwd.shape[0]
    cells, ny, nz = logc.shape
    f32 = jnp.float32
    anywhere, far, vmem = pl.BlockSpec(memory_space=pl.ANY), pl.BlockSpec(memory_space=pltpu.HBM), pl.BlockSpec(memory_space=pltpu.VMEM)
    dma = pltpu.SemaphoreType.DMA
    return pl.pallas_call(
        functools.partial(field_kernel, n),
        out_shape=(
            jax.ShapeDtypeStruct(adj.shape, f32),
            jax.ShapeDtypeStruct((cells, ny, 2 * nz), jnp.bfloat16),
            jax.ShapeDtypeStruct(model.shape, f32),
        ),
        in_specs=[far] * 5 + [pl.BlockSpec(memory_space=pltpu.SMEM), far, far],
        out_specs=(anywhere, vmem, vmem),
        scratch_shapes=[
            pltpu.VMEM(spacing.shape, f32),
            pltpu.VMEM(residuals.shape, f32),
            pltpu.VMEM(counts.shape, jnp.int32),
            pltpu.VMEM(model.shape, f32),
            pltpu.VMEM((3, cells, ny + 8, nz), f32),
            pltpu.VMEM((3, cells + 1, ny + 8, nz), f32),
            pltpu.VMEM((cells, ny, nz), f32),
            pltpu.VMEM((cells, ny, nz), f32),
            pltpu.VMEM((cells, ny, nz), f32),
            pltpu.VMEM(fwd.shape, jnp.bfloat16),
            pltpu.VMEM((ny, nz), f32),
            pltpu.VMEM((steps, 2, ny, nz), f32),
            pltpu.VMEM((steps, 2, ny, nz), f32),
            pltpu.VMEM((steps, 2, ny, nz), f32),
            pltpu.VMEM((model.shape[0], ny + 16, nz), f32),
            pltpu.VMEM((ny, nz), f32),
            pltpu.VMEM((ny, nz), f32),
            dma((10,)),
            dma((steps,)),
            dma((steps,)),
            dma((steps,)),
            dma((steps,)),
            dma((steps,)),
            dma((2,)),
            dma((2,)),
        ],
        compiler_params=pltpu.CompilerParams(collective_id=0, has_side_effects=True, vmem_limit_bytes=60 << 20),
    )(adj, fwd, logc, spacing, residuals, gates, counts, model)


def relayout_kernel(
    n,
    sens_hbm,
    voxel_hbm,
    reg_hbm,
    out_ref,
    sens,
    voxel,
    ids,
    reg,
    to_pair,
    from_pair,
    across,
    from_across,
    held,
    arrived,
    load_sem,
    pair_send,
    pair_recv,
    across_send,
    across_recv,
    layer_send,
    layer_recv,
):
    layers = n // 4
    cells, ny = voxel_hbm.shape
    voxels, nz = reg_hbm.shape
    blocks, size = 2 * layers, voxels // 2
    grp, me = lax.axis_index("grp"), lax.axis_index("tx")
    core, half, layer = lax.rem(me, 2), lax.rem(me // 2, 2), me // 4
    up = jnp.where(layer < layers // 2, 1, 0)

    def tile(z, y, c):
        return (z * 2 + y) * 2 + c

    def layer_at(k):
        return up * (layers - 1 - k) + (1 - up) * k

    loads = [
        pltpu.make_async_copy(source, target, load_sem.at[i])
        for i, (source, target) in enumerate(((sens_hbm, sens), (voxel_hbm, voxel), (reg_hbm, reg)))
    ]
    for copy in loads:
        copy.start()
    barrier = pltpu.get_barrier_semaphore()
    for other in (tile(layer, half, 1 - core), tile(layer, 1 - half, core)):
        pl.semaphore_signal(barrier, inc=1, device_id=(grp, other), device_id_type=MESH)

    def greet(z, carry):
        @pl.when(z != layer)
        def _():
            pl.semaphore_signal(
                barrier, inc=1, device_id=(grp, tile(z, half, core)), device_id_type=MESH
            )

        return carry

    lax.fori_loop(0, layers, greet, 0)
    for copy in loads:
        copy.wait()
    for x in range(cells):
        ids[:, x * ny : (x + 1) * ny] = voxel[x : x + 1, :]

    def pair_copy(k, y):
        return pltpu.make_async_remote_copy(
            src_ref=to_pair.at[k, y],
            dst_ref=from_pair.at[k, y],
            send_sem=pair_send.at[k, y],
            recv_sem=pair_recv.at[k, y],
            device_id=(grp, tile(layer, half, 1 - core)),
            device_id_type=MESH,
        )

    def across_copy(k):
        return pltpu.make_async_remote_copy(
            src_ref=across.at[k],
            dst_ref=from_across.at[k],
            send_sem=across_send.at[k],
            recv_sem=across_recv.at[k],
            device_id=(grp, tile(layer, 1 - half, core)),
            device_id_type=MESH,
        )

    def layer_copy(k):
        return pltpu.make_async_remote_copy(
            src_ref=held.at[k],
            dst_ref=arrived.at[layer, lax.rem(k, 2)],
            send_sem=layer_send.at[k],
            recv_sem=layer_recv.at[layer, lax.rem(k, 2)],
            device_id=(grp, tile(layer_at(k // 2), half, core)),
            device_id_type=MESH,
        )

    def arrival(z, part):
        return pltpu.make_async_remote_copy(
            src_ref=held.at[0],
            dst_ref=arrived.at[z, part],
            send_sem=layer_send.at[0],
            recv_sem=layer_recv.at[z, part],
            device_id=(grp, tile(z, half, core)),
            device_id_type=MESH,
        )

    def target_sums(k, y, c):
        first = tile(layer_at(k // 2), y, c) * voxels + lax.rem(k, 2) * size
        here = lax.broadcasted_iota(jnp.int32, (size, cells * ny), 0) == ids[...] - first
        picked = jnp.where(here, 1.0, 0.0).astype(jnp.bfloat16)
        sums = jnp.dot(picked, sens[...], preferred_element_type=jnp.float32)
        return sums[:, 0:nz] + sums[:, nz : 2 * nz]

    def forward(k):
        across_copy(k).wait_recv()
        pair_copy(k, 1).wait_recv()
        held[k] = held[k] + from_pair[k, 1] + from_across[k]

        @pl.when(layer_at(k // 2) != layer)
        def _():
            layer_copy(k).start()

    def stage(k, carry):
        across[k] = target_sums(k, 1 - half, core)
        pair_copy(k, 0).wait_recv()
        across[k] = across[k] + from_pair[k, 0]
        across_copy(k).start()

        @pl.when(k < blocks - 1)
        def _():
            to_pair[k + 1, 0] = target_sums(k + 1, 1 - half, 1 - core)
            pair_copy(k + 1, 0).start()

        to_pair[k, 1] = target_sums(k, half, 1 - core)
        pair_copy(k, 1).start()
        held[k] = target_sums(k, half, core)

        @pl.when(k > 0)
        def _():
            forward(k - 1)

        return carry

    to_pair[0, 0] = target_sums(0, 1 - half, 1 - core)
    pl.semaphore_wait(barrier, layers + 1)
    pair_copy(0, 0).start()
    lax.fori_loop(0, blocks, stage, 0)
    forward(blocks - 1)
    own = up * (layers - 1 - layer) + (1 - up) * layer
    for part in range(2):
        at = pl.ds(part * size, size)
        out_ref[at, :] = reg[at, :] + held[2 * own + part]

    def collect(z, carry):
        @pl.when(z != layer)
        def _():
            for part in range(2):
                at = pl.ds(part * size, size)
                arrival(z, part).wait_recv()
                out_ref[at, :] = out_ref[at, :] + arrived[z, part]

        return carry

    lax.fori_loop(0, layers, collect, 0)

    def drain(k, carry):
        pair_copy(k, 0).wait_send()
        pair_copy(k, 1).wait_send()
        across_copy(k).wait_send()

        @pl.when(layer_at(k // 2) != layer)
        def _():
            layer_copy(k).wait_send()

        return carry

    lax.fori_loop(0, blocks, drain, 0)


def relayout(n, sensitivity, voxel_column, regularity):
    cells, ny = voxel_column.shape
    nz = regularity.shape[2]
    voxels = regularity.shape[0] * regularity.shape[1]
    layers = n // 4
    f32, dma = jnp.float32, pltpu.SemaphoreType.DMA
    far = pl.BlockSpec(memory_space=pltpu.HBM)
    block, part = (voxels, nz), (voxels // 2, nz)
    blocks = 2 * layers
    out = pl.pallas_call(
        functools.partial(relayout_kernel, n),
        out_shape=jax.ShapeDtypeStruct(block, f32),
        in_specs=[far] * 3,
        out_specs=pl.BlockSpec(memory_space=pltpu.VMEM),
        scratch_shapes=[
            pltpu.VMEM((cells * ny, 2 * nz), jnp.bfloat16),
            pltpu.VMEM((cells, ny), jnp.int32),
            pltpu.VMEM((1, cells * ny), jnp.int32),
            pltpu.VMEM(block, f32),
            pltpu.VMEM((blocks, 2) + part, f32),
            pltpu.VMEM((blocks, 2) + part, f32),
            pltpu.VMEM((blocks,) + part, f32),
            pltpu.VMEM((blocks,) + part, f32),
            pltpu.VMEM((blocks,) + part, f32),
            pltpu.VMEM((layers, 2) + part, f32),
            dma((3,)),
            dma((blocks, 2)),
            dma((blocks, 2)),
            dma((blocks,)),
            dma((blocks,)),
            dma((blocks,)),
            dma((layers, 2)),
        ],
        compiler_params=pltpu.CompilerParams(collective_id=1, has_side_effects=True, vmem_limit_bytes=60 << 20),
    )(sensitivity.reshape(cells * ny, 2 * nz), voxel_column, regularity.reshape(block))
    return out.reshape(regularity.shape)


def body(
    adjoint_in,
    forward_terms,
    log_conductivity,
    spacing,
    residuals,
    gate_index,
    counts,
    voxel_column,
    voxel_model,
):
    tile_count = lax.axis_size("tx")
    adjoint, sensitivity, regularity = field_phase(
        tile_count,
        adjoint_in,
        forward_terms,
        log_conductivity,
        spacing,
        residuals,
        gate_index,
        counts,
        voxel_model,
    )
    gradient = relayout(tile_count, sensitivity, voxel_column, regularity)
    return (adjoint, gradient)


def solution(mesh):
    in_specs = (
        P(None, ("grp", "tx"), None, None),
        P(None, None, ("grp", "tx"), None, None),
        P(("grp", "tx"), None, None),
        P(("grp", "tx"), None),
        P(None, ("grp", "tx"), None),
        P("grp"),
        P(("grp", "tx"), None),
        P(("grp", "tx"), None),
        P(("grp", "tx"), None, None),
    )
    out_specs = (P(None, ("grp", "tx"), None, None), P(("grp", "tx"), None, None))
    return jax.shard_map(body, mesh=mesh, in_specs=in_specs, out_specs=out_specs, check_vma=False)
```

```python
import functools

import jax
import jax.numpy as jnp
from jax import lax
from jax.experimental import pallas as pl
from jax.experimental.pallas import tpu as pltpu
from jax.sharding import PartitionSpec as P

MESH = pl.DeviceIdType.MESH


def lane_index(shape):
    return lax.broadcasted_iota(jnp.int32, shape, 1)


def next_z(value):
    depth = value.shape[1]
    return jnp.where(lane_index(value.shape) < depth - 1, pltpu.roll(value, depth - 1, 1), 0.0)


def last_z(value):
    return jnp.where(lane_index(value.shape) > 0, pltpu.roll(value, 1, 1), 0.0)


def field_kernel(
    n,
    adj_ref,
    fwd_ref,
    logc_ref,
    spacing_hbm,
    residual_hbm,
    gate_ref,
    counts_hbm,
    model_hbm,
    out_ref,
    sens_ref,
    reg_ref,
    spacing_ref,
    residual_ref,
    counts_ref,
    model_ref,
    field,
    curl,
    coef,
    inv,
    total,
    terms,
    columns,
    from_low,
    from_high,
    to_high,
    model,
    model_low,
    model_high,
    local_sem,
    term_sem,
    send_up,
    send_down,
    recv_low,
    recv_high,
    model_send,
    model_recv,
):
    steps = fwd_ref.shape[0]
    cells, ny, nz = logc_ref.shape
    rows_v = model_hbm.shape[0]
    grp, me = lax.axis_index("grp"), lax.axis_index("tx")
    low, high = lax.rem(me + n - 1, n), lax.rem(me + 1, n)
    has_low, has_high = me > 0, me < n - 1
    chunk = 64


    def pieces(first, last):
        return [(y, min(chunk, last - y)) for y in range(first, last, chunk)]

    chunks = pieces(0, ny)

    def halves(slot):
        middle = ny // 2 + 8 * (1 - slot)
        return ((0, middle), (middle, ny))

    small = [
        pltpu.make_async_copy(source, target, local_sem.at[6 + i])
        for i, (source, target) in enumerate(
            (
                (spacing_hbm, spacing_ref),
                (counts_hbm, counts_ref),
                (residual_hbm, residual_ref),
                (model_hbm, model_ref),
            )
        )
    ]
    for copy in small[:3]:
        copy.start()
    load_last = pltpu.make_async_copy(
        adj_ref.at[:, pl.ds(cells - 1, 1)], field.at[:, pl.ds(cells - 1, 1), pl.ds(0, ny)], local_sem.at[0]
    )
    load_last.start()
    load_rest = pltpu.make_async_copy(
        adj_ref.at[:, pl.ds(0, cells - 1)], field.at[:, pl.ds(0, cells - 1), pl.ds(0, ny)], local_sem.at[1]
    )
    load_rest.start()
    load_coef = pltpu.make_async_copy(logc_ref, coef, local_sem.at[2])
    load_coef.start()
    load_terms = [pltpu.make_async_copy(fwd_ref.at[s], terms.at[s], term_sem.at[s]) for s in range(steps)]
    for copy in load_terms:
        copy.start()
    small[3].start()

    barrier = pltpu.get_barrier_semaphore()
    for neighbour in (low, high):
        pl.semaphore_signal(barrier, inc=1, device_id=(grp, neighbour), device_id_type=MESH)

    for copy in small[:3]:
        copy.wait()
    inverse = 1.0 / spacing_ref[...]
    depth_count = counts_ref[...].astype(jnp.float32)
    sources = [residual_ref[gate_ref[s]] for s in range(steps)]
    for y in range(0, ny, nz):
        parts = [v[:, y : y + nz] for v in [inverse, depth_count] + sources]
        parts.append(jnp.zeros((nz - cells * (2 + steps), nz), jnp.float32))
        columns[pl.ds(y, nz), :] = jnp.concatenate(parts, axis=0).T

    for x in range(cells):
        inv[x] = jnp.broadcast_to(columns[:, x : x + 1], (ny, nz))
        for a in range(3):
            field[a, x, pl.ds(ny, 8), :] = jnp.zeros((8, nz), jnp.float32)
            curl[a, x + 1, pl.ds(0, 8), :] = jnp.zeros((8, nz), jnp.float32)

    def copy_up(slot, part):
        first, last = halves(slot)[part]
        at = pl.ds(first, last - first)
        return pltpu.make_async_remote_copy(
            src_ref=to_high.at[slot, :, at],
            dst_ref=from_low.at[slot, :, at],
            send_sem=send_up.at[slot, part],
            recv_sem=recv_low.at[slot, part],
            device_id=(grp, high),
            device_id_type=MESH,
        )

    def copy_down(slot, part):
        first, last = halves(slot)[part]
        at = pl.ds(first, last - first)
        origin = adj_ref if slot == 0 else field
        return pltpu.make_async_remote_copy(
            src_ref=origin.at[pl.ds(1, 2), 0, at],
            dst_ref=from_high.at[slot, :, at],
            send_sem=send_down.at[slot, part],
            recv_sem=recv_high.at[slot, part],
            device_id=(grp, low),
            device_id_type=MESH,
        )

    def send_high(slot, part):
        x = cells - 1
        for y, size in pieces(*halves(slot)[part]):
            e0, e1, e2 = (field[a, x, pl.ds(y, size), :] for a in range(3))
            e0y = field[0, x, pl.ds(y + 1, size), :]
            to_high[slot, 0, pl.ds(y, size), :] = inv[x, pl.ds(y, size), :] * (next_z(e0) - e0) + e2
            to_high[slot, 1, pl.ds(y, size), :] = (e0 - e0y) - e1

        @pl.when(has_high)
        def _():
            copy_up(slot, part).start()

    def send_low(slot, part):
        @pl.when(has_low)
        def _():
            copy_down(slot, part).start()

    def curl_row(x, next_row, where=chunks):
        for y, size in where:
            at = pl.ds(y, size)
            e0, e1, e2 = (field[a, x, at, :] for a in range(3))
            e0y, e2y = field[0, x, pl.ds(y + 1, size), :], field[2, x, pl.ds(y + 1, size), :]
            e1x, e2x = next_row(at)
            h = inv[x, at, :]
            to = pl.ds(y + 8, size)
            curl[0, x + 1, to, :] = (e2y - e2) - h * (next_z(e1) - e1)
            curl[1, x + 1, to, :] = h * (next_z(e0) - e0) - (e2x - e2)
            curl[2, x + 1, to, :] = (e1x - e1) - (e0y - e0)

    def update_row(s, x, where=chunks):
        for y, size in where:
            at, to, before = pl.ds(y, size), pl.ds(y + 8, size), pl.ds(y + 7, size)
            h, c = inv[x, at, :], coef[x, at, :]
            h0, h1, h2 = (curl[a, x + 1, to, :] for a in range(3))
            h0y, h2y = curl[0, x + 1, before, :], curl[2, x + 1, before, :]
            h1x, h2x = curl[1, x, to, :], curl[2, x, to, :]
            image = (
                (h2 - h2y) - h * (h1 - last_z(h1)),
                h * (h0 - last_z(h0)) - (h2 - h2x),
                (h1 - h1x) - (h0 - h0y),
            )
            shift = nz - 1 - (2 + s) * cells - x
            source = pltpu.roll(columns[at, :], shift, 1)
            source = jnp.where(lane_index(source.shape) == nz - 1, source, 0.0)
            for a in range(3):
                value = field[a, x, at, :] - c * image[a]
                field[a, x, at, :] = value + source if a == 2 else value

    def product_row(s, x):
        for y, size in chunks:
            at = pl.ds(y, size)
            value = sum(field[a, x, at, :] * terms[s, a, x, at, :].astype(jnp.float32) for a in range(3))
            total[x, at, :] = value if s == 0 else total[x, at, :] + value

    pl.semaphore_wait(barrier, 2)
    send_low(0, 0)
    load_last.wait()
    send_high(0, 0)
    send_low(0, 1)
    send_high(0, 1)
    load_rest.wait()

    def model_up():
        return pltpu.make_async_remote_copy(
            src_ref=model_hbm.at[rows_v - 1],
            dst_ref=model_low,
            send_sem=model_send.at[0],
            recv_sem=model_recv.at[0],
            device_id=(grp, high),
            device_id_type=MESH,
        )

    def model_down():
        return pltpu.make_async_remote_copy(
            src_ref=model_hbm.at[0],
            dst_ref=model_high,
            send_sem=model_send.at[1],
            recv_sem=model_recv.at[1],
            device_id=(grp, low),
            device_id_type=MESH,
        )

    @pl.when(has_high)
    def _():
        model_up().start()

    @pl.when(has_low)
    def _():
        model_down().start()

    load_coef.wait()

    def coefficient_row(x, carry):
        coef[x] = 0.05 * jnp.exp(-0.7 * coef[x])
        return carry

    lax.fori_loop(0, cells, coefficient_row, 0)

    @pl.when(jnp.logical_not(has_low))
    def _():
        model_low[...] = jnp.zeros_like(model_low)

    @pl.when(jnp.logical_not(has_high))
    def _():
        model_high[...] = jnp.zeros_like(model_high)
        for s in range(steps):
            from_high[s] = jnp.zeros(from_high.shape[1:], jnp.float32)

    def regularize():
        @pl.when(has_high)
        def _():
            model_up().wait_send()
            model_down().wait_recv()

        @pl.when(has_low)
        def _():
            model_down().wait_send()
            model_up().wait_recv()

        small[3].wait()
        for v in range(rows_v):
            model[v, pl.ds(0, 8), :] = jnp.zeros((8, nz), jnp.float32)
            model[v, pl.ds(ny + 8, 8), :] = jnp.zeros((8, nz), jnp.float32)
            model[v, pl.ds(8, ny), :] = model_ref[v]
        for v in range(rows_v):
            for y, size in chunks:
                at = pl.ds(y, size)
                center = model_ref[v, at, :]
                below = model_low[at, :] if v == 0 else model_ref[v - 1, at, :]
                above = model_high[at, :] if v == rows_v - 1 else model_ref[v + 1, at, :]
                sides = model[v, pl.ds(y + 7, size), :] + model[v, pl.ds(y + 9, size), :]
                around = below + above + sides + next_z(center) + last_z(center)
                reg_ref[v, at, :] = 0.1 * (6.0 * center - around)

    def store(first, count, sem):
        return pltpu.make_async_copy(
            field.at[:, pl.ds(first, count), pl.ds(0, ny)], out_ref.at[:, pl.ds(first, count)], local_sem.at[sem]
        )

    def sensitivity_row(x, carry):
        product_row(steps - 1, x)
        limit = pltpu.roll(columns[...], nz - cells - x, 1)
        limit = jnp.broadcast_to(limit[:, 0:1], (ny, nz))
        inside = lane_index((ny, nz)).astype(jnp.float32) < limit
        sens = jnp.where(inside, -0.7 * coef[x] * total[x], 0.0)
        coarse = sens.astype(jnp.bfloat16)
        sens_ref[x, :, 0:nz] = coarse
        sens_ref[x, :, nz : 2 * nz] = (sens - coarse.astype(jnp.float32)).astype(jnp.bfloat16)
        return carry

    for s in range(steps):

        def inner_curl(x, carry):
            curl_row(x, lambda at: (field[1, x + 1, at, :], field[2, x + 1, at, :]))
            return carry

        lax.fori_loop(0, cells - 1, inner_curl, 0)
        if s > 0:

            def late_product(x, carry):
                product_row(s - 1, x)
                return carry

            load_terms[s - 1].wait()
            lax.fori_loop(0, cells, late_product, 0)

        def inner_update(x, carry):
            update_row(s, x)
            return carry

        lax.fori_loop(1, cells - 1, inner_update, 0)
        if s == steps - 1:
            store(1, cells - 2, 3).start()
        if s == min(1, steps - 1):
            regularize()

        if s == steps - 1:
            load_terms[s].wait()
            lax.fori_loop(1, cells - 1, sensitivity_row, 0)
        for part, (first, last) in enumerate(halves(s)):
            where = pieces(first, last)

            @pl.when(has_high)
            def _():
                copy_up(s, part).wait_send()
                copy_down(s, part).wait_recv()

            curl_row(cells - 1, lambda at: (from_high[s, 0, at, :], from_high[s, 1, at, :]), where)
            update_row(s, cells - 1, where)
            if s < steps - 1:
                send_high(s + 1, part)

            @pl.when(has_low)
            def _():
                copy_down(s, part).wait_send()
                copy_up(s, part).wait_recv()
                for y, size in where:
                    at, to = pl.ds(y, size), pl.ds(y + 8, size)
                    curl[1, 0, to, :] = from_low[s, 0, at, :] - field[2, 0, at, :]
                    curl[2, 0, to, :] = from_low[s, 1, at, :] + field[1, 0, at, :]

            @pl.when(jnp.logical_not(has_low))
            def _():
                for a in (1, 2):
                    curl[a, 0, pl.ds(first + 8, last - first), :] = jnp.zeros((last - first, nz), jnp.float32)

            update_row(s, 0, where)
            if s < steps - 1:
                send_low(s + 1, part)
    store(0, 1, 4).start()
    store(cells - 1, 1, 5).start()

    sensitivity_row(0, 0)
    sensitivity_row(cells - 1, 0)
    store(1, cells - 2, 3).wait()
    store(0, 1, 4).wait()
    store(cells - 1, 1, 5).wait()


def field_phase(n, adj, fwd, logc, spacing, residuals, gates, counts, model):
    steps = fwd.shape[0]
    cells, ny, nz = logc.shape
    f32 = jnp.float32
    anywhere, far, vmem = pl.BlockSpec(memory_space=pl.ANY), pl.BlockSpec(memory_space=pltpu.HBM), pl.BlockSpec(memory_space=pltpu.VMEM)
    dma = pltpu.SemaphoreType.DMA
    return pl.pallas_call(
        functools.partial(field_kernel, n),
        out_shape=(
            jax.ShapeDtypeStruct(adj.shape, f32),
            jax.ShapeDtypeStruct((cells, ny, 2 * nz), jnp.bfloat16),
            jax.ShapeDtypeStruct(model.shape, f32),
        ),
        in_specs=[far] * 5 + [pl.BlockSpec(memory_space=pltpu.SMEM), far, far],
        out_specs=(anywhere, vmem, vmem),
        scratch_shapes=[
            pltpu.VMEM(spacing.shape, f32),
            pltpu.VMEM(residuals.shape, f32),
            pltpu.VMEM(counts.shape, jnp.int32),
            pltpu.VMEM(model.shape, f32),
            pltpu.VMEM((3, cells, ny + 8, nz), f32),
            pltpu.VMEM((3, cells + 1, ny + 8, nz), f32),
            pltpu.VMEM((cells, ny, nz), f32),
            pltpu.VMEM((cells, ny, nz), f32),
            pltpu.VMEM((cells, ny, nz), f32),
            pltpu.VMEM(fwd.shape, jnp.bfloat16),
            pltpu.VMEM((ny, nz), f32),
            pltpu.VMEM((steps, 2, ny, nz), f32),
            pltpu.VMEM((steps, 2, ny, nz), f32),
            pltpu.VMEM((steps, 2, ny, nz), f32),
            pltpu.VMEM((model.shape[0], ny + 16, nz), f32),
            pltpu.VMEM((ny, nz), f32),
            pltpu.VMEM((ny, nz), f32),
            dma((10,)),
            dma((steps,)),
            dma((steps, 2)),
            dma((steps, 2)),
            dma((steps, 2)),
            dma((steps, 2)),
            dma((2,)),
            dma((2,)),
        ],
        compiler_params=pltpu.CompilerParams(collective_id=0, has_side_effects=True, vmem_limit_bytes=60 << 20),
    )(adj, fwd, logc, spacing, residuals, gates, counts, model)


def relayout_kernel(
    n,
    sens_hbm,
    voxel_hbm,
    reg_hbm,
    out_ref,
    sens,
    voxel,
    ids,
    reg,
    to_pair,
    from_pair,
    across,
    from_across,
    held,
    arrived,
    load_sem,
    pair_send,
    pair_recv,
    across_send,
    across_recv,
    layer_send,
    layer_recv,
):
    layers = n // 4
    cells, ny = voxel_hbm.shape
    voxels, nz = reg_hbm.shape
    blocks, size = 2 * layers, voxels // 2
    grp, me = lax.axis_index("grp"), lax.axis_index("tx")
    core, half, layer = lax.rem(me, 2), lax.rem(me // 2, 2), me // 4
    up = jnp.where(layer < layers // 2, 1, 0)

    def tile(z, y, c):
        return (z * 2 + y) * 2 + c

    def layer_at(k):
        return up * (layers - 1 - k) + (1 - up) * k

    loads = [
        pltpu.make_async_copy(source, target, load_sem.at[i])
        for i, (source, target) in enumerate(((sens_hbm, sens), (voxel_hbm, voxel), (reg_hbm, reg)))
    ]
    for copy in loads:
        copy.start()
    barrier = pltpu.get_barrier_semaphore()
    for other in (tile(layer, half, 1 - core), tile(layer, 1 - half, core)):
        pl.semaphore_signal(barrier, inc=1, device_id=(grp, other), device_id_type=MESH)

    def greet(z, carry):
        @pl.when(z != layer)
        def _():
            pl.semaphore_signal(
                barrier, inc=1, device_id=(grp, tile(z, half, core)), device_id_type=MESH
            )

        return carry

    lax.fori_loop(0, layers, greet, 0)
    for copy in loads:
        copy.wait()
    for x in range(cells):
        ids[:, x * ny : (x + 1) * ny] = voxel[x : x + 1, :]

    def pair_copy(k, y):
        return pltpu.make_async_remote_copy(
            src_ref=to_pair.at[k, y],
            dst_ref=from_pair.at[k, y],
            send_sem=pair_send.at[k, y],
            recv_sem=pair_recv.at[k, y],
            device_id=(grp, tile(layer, half, 1 - core)),
            device_id_type=MESH,
        )

    def across_copy(k):
        return pltpu.make_async_remote_copy(
            src_ref=across.at[k],
            dst_ref=from_across.at[k],
            send_sem=across_send.at[k],
            recv_sem=across_recv.at[k],
            device_id=(grp, tile(layer, 1 - half, core)),
            device_id_type=MESH,
        )

    def layer_copy(k):
        return pltpu.make_async_remote_copy(
            src_ref=held.at[k],
            dst_ref=arrived.at[layer, lax.rem(k, 2)],
            send_sem=layer_send.at[k],
            recv_sem=layer_recv.at[layer, lax.rem(k, 2)],
            device_id=(grp, tile(layer_at(k // 2), half, core)),
            device_id_type=MESH,
        )

    def arrival(z, part):
        return pltpu.make_async_remote_copy(
            src_ref=held.at[0],
            dst_ref=arrived.at[z, part],
            send_sem=layer_send.at[0],
            recv_sem=layer_recv.at[z, part],
            device_id=(grp, tile(z, half, core)),
            device_id_type=MESH,
        )

    def target_sums(k, y, c):
        first = tile(layer_at(k // 2), y, c) * voxels + lax.rem(k, 2) * size
        here = lax.broadcasted_iota(jnp.int32, (size, cells * ny), 0) == ids[...] - first
        picked = jnp.where(here, 1.0, 0.0).astype(jnp.bfloat16)
        sums = jnp.dot(picked, sens[...], preferred_element_type=jnp.float32)
        return sums[:, 0:nz] + sums[:, nz : 2 * nz]

    def forward(k):
        across_copy(k).wait_recv()
        pair_copy(k, 1).wait_recv()
        held[k] = held[k] + from_pair[k, 1] + from_across[k]

        @pl.when(layer_at(k // 2) != layer)
        def _():
            layer_copy(k).start()

    def stage(k, carry):
        across[k] = target_sums(k, 1 - half, core)
        pair_copy(k, 0).wait_recv()
        across[k] = across[k] + from_pair[k, 0]
        across_copy(k).start()

        @pl.when(k < blocks - 1)
        def _():
            to_pair[k + 1, 0] = target_sums(k + 1, 1 - half, 1 - core)
            pair_copy(k + 1, 0).start()

        to_pair[k, 1] = target_sums(k, half, 1 - core)
        pair_copy(k, 1).start()
        held[k] = target_sums(k, half, core)

        @pl.when(k > 0)
        def _():
            forward(k - 1)

        return carry

    to_pair[0, 0] = target_sums(0, 1 - half, 1 - core)
    pl.semaphore_wait(barrier, layers + 1)
    pair_copy(0, 0).start()
    lax.fori_loop(0, blocks, stage, 0)
    forward(blocks - 1)
    own = up * (layers - 1 - layer) + (1 - up) * layer
    for part in range(2):
        at = pl.ds(part * size, size)
        out_ref[at, :] = reg[at, :] + held[2 * own + part]

    def collect(z, carry):
        @pl.when(z != layer)
        def _():
            for part in range(2):
                at = pl.ds(part * size, size)
                arrival(z, part).wait_recv()
                out_ref[at, :] = out_ref[at, :] + arrived[z, part]

        return carry

    lax.fori_loop(0, layers, collect, 0)

    def drain(k, carry):
        pair_copy(k, 0).wait_send()
        pair_copy(k, 1).wait_send()
        across_copy(k).wait_send()

        @pl.when(layer_at(k // 2) != layer)
        def _():
            layer_copy(k).wait_send()

        return carry

    lax.fori_loop(0, blocks, drain, 0)


def relayout(n, sensitivity, voxel_column, regularity):
    cells, ny = voxel_column.shape
    nz = regularity.shape[2]
    voxels = regularity.shape[0] * regularity.shape[1]
    layers = n // 4
    f32, dma = jnp.float32, pltpu.SemaphoreType.DMA
    far = pl.BlockSpec(memory_space=pltpu.HBM)
    block, part = (voxels, nz), (voxels // 2, nz)
    blocks = 2 * layers
    out = pl.pallas_call(
        functools.partial(relayout_kernel, n),
        out_shape=jax.ShapeDtypeStruct(block, f32),
        in_specs=[far] * 3,
        out_specs=pl.BlockSpec(memory_space=pltpu.VMEM),
        scratch_shapes=[
            pltpu.VMEM((cells * ny, 2 * nz), jnp.bfloat16),
            pltpu.VMEM((cells, ny), jnp.int32),
            pltpu.VMEM((1, cells * ny), jnp.int32),
            pltpu.VMEM(block, f32),
            pltpu.VMEM((blocks, 2) + part, f32),
            pltpu.VMEM((blocks, 2) + part, f32),
            pltpu.VMEM((blocks,) + part, f32),
            pltpu.VMEM((blocks,) + part, f32),
            pltpu.VMEM((blocks,) + part, f32),
            pltpu.VMEM((layers, 2) + part, f32),
            dma((3,)),
            dma((blocks, 2)),
            dma((blocks, 2)),
            dma((blocks,)),
            dma((blocks,)),
            dma((blocks,)),
            dma((layers, 2)),
        ],
        compiler_params=pltpu.CompilerParams(collective_id=1, has_side_effects=True, vmem_limit_bytes=60 << 20),
    )(sensitivity.reshape(cells * ny, 2 * nz), voxel_column, regularity.reshape(block))
    return out.reshape(regularity.shape)


def body(
    adjoint_in,
    forward_terms,
    log_conductivity,
    spacing,
    residuals,
    gate_index,
    counts,
    voxel_column,
    voxel_model,
):
    tile_count = lax.axis_size("tx")
    adjoint, sensitivity, regularity = field_phase(
        tile_count,
        adjoint_in,
        forward_terms,
        log_conductivity,
        spacing,
        residuals,
        gate_index,
        counts,
        voxel_model,
    )
    gradient = relayout(tile_count, sensitivity, voxel_column, regularity)
    return (adjoint, gradient)


def solution(mesh):
    in_specs = (
        P(None, ("grp", "tx"), None, None),
        P(None, None, ("grp", "tx"), None, None),
        P(("grp", "tx"), None, None),
        P(("grp", "tx"), None),
        P(None, ("grp", "tx"), None),
        P("grp"),
        P(("grp", "tx"), None),
        P(("grp", "tx"), None),
        P(("grp", "tx"), None, None),
    )
    out_specs = (P(None, ("grp", "tx"), None, None), P(("grp", "tx"), None, None))
    return jax.shard_map(body, mesh=mesh, in_specs=in_specs, out_specs=out_specs, check_vma=False)
```

```python
import functools

import jax
import jax.numpy as jnp
from jax import lax
from jax.experimental import pallas as pl
from jax.experimental.pallas import tpu as pltpu
from jax.sharding import PartitionSpec as P

MESH = pl.DeviceIdType.MESH


def lane_index(shape):
    return lax.broadcasted_iota(jnp.int32, shape, 1)


def next_z(value):
    depth = value.shape[1]
    return jnp.where(lane_index(value.shape) < depth - 1, pltpu.roll(value, depth - 1, 1), 0.0)


def last_z(value):
    return jnp.where(lane_index(value.shape) > 0, pltpu.roll(value, 1, 1), 0.0)


def field_kernel(
    n,
    adj_ref,
    fwd_ref,
    logc_ref,
    spacing_hbm,
    residual_hbm,
    gate_ref,
    counts_hbm,
    model_hbm,
    out_ref,
    sens_ref,
    reg_ref,
    spacing_ref,
    residual_ref,
    counts_ref,
    model_ref,
    field,
    curl,
    coef,
    inv,
    total,
    terms,
    columns,
    from_low,
    from_high,
    to_high,
    model,
    model_low,
    model_high,
    local_sem,
    term_sem,
    send_up,
    send_down,
    recv_low,
    recv_high,
    model_send,
    model_recv,
):
    steps = fwd_ref.shape[0]
    cells, ny, nz = logc_ref.shape
    rows_v = model_hbm.shape[0]
    grp, me = lax.axis_index("grp"), lax.axis_index("tx")
    low, high = lax.rem(me + n - 1, n), lax.rem(me + 1, n)
    has_low, has_high = me > 0, me < n - 1
    chunk = 64


    def pieces(first, last):
        return [(y, min(chunk, last - y)) for y in range(first, last, chunk)]

    chunks = pieces(0, ny)

    def halves(slot):
        middle = ny // 2 + 8 * (1 - slot)
        return ((0, middle), (middle, ny))

    small = [
        pltpu.make_async_copy(source, target, local_sem.at[6 + i])
        for i, (source, target) in enumerate(
            (
                (spacing_hbm, spacing_ref),
                (counts_hbm, counts_ref),
                (residual_hbm, residual_ref),
                (model_hbm, model_ref),
            )
        )
    ]
    for copy in small[:3]:
        copy.start()
    load_last = pltpu.make_async_copy(
        adj_ref.at[:, pl.ds(cells - 1, 1)], field.at[:, pl.ds(cells - 1, 1), pl.ds(0, ny)], local_sem.at[0]
    )
    load_last.start()
    load_rest = pltpu.make_async_copy(
        adj_ref.at[:, pl.ds(0, cells - 1)], field.at[:, pl.ds(0, cells - 1), pl.ds(0, ny)], local_sem.at[1]
    )
    load_rest.start()
    load_coef = pltpu.make_async_copy(logc_ref, coef, local_sem.at[2])
    load_coef.start()
    load_terms = [pltpu.make_async_copy(fwd_ref.at[s], terms.at[s], term_sem.at[s]) for s in range(steps)]
    for copy in load_terms:
        copy.start()
    small[3].start()

    barrier = pltpu.get_barrier_semaphore()
    for neighbour in (low, high):
        pl.semaphore_signal(barrier, inc=1, device_id=(grp, neighbour), device_id_type=MESH)

    for copy in small[:3]:
        copy.wait()
    inverse = 1.0 / spacing_ref[...]
    depth_count = counts_ref[...].astype(jnp.float32)
    sources = [residual_ref[gate_ref[s]] for s in range(steps)]
    for y in range(0, ny, nz):
        parts = [v[:, y : y + nz] for v in [inverse, depth_count] + sources]
        parts.append(jnp.zeros((nz - cells * (2 + steps), nz), jnp.float32))
        columns[pl.ds(y, nz), :] = jnp.concatenate(parts, axis=0).T

    for x in range(cells):
        inv[x] = jnp.broadcast_to(columns[:, x : x + 1], (ny, nz))
        for a in range(3):
            field[a, x, pl.ds(ny, 8), :] = jnp.zeros((8, nz), jnp.float32)
            curl[a, x + 1, pl.ds(0, 8), :] = jnp.zeros((8, nz), jnp.float32)

    def copy_up(slot, part):
        first, last = halves(slot)[part]
        at = pl.ds(first, last - first)
        return pltpu.make_async_remote_copy(
            src_ref=to_high.at[slot, :, at],
            dst_ref=from_low.at[slot, :, at],
            send_sem=send_up.at[slot, part],
            recv_sem=recv_low.at[slot, part],
            device_id=(grp, high),
            device_id_type=MESH,
        )

    def copy_down(slot, part):
        first, last = halves(slot)[part]
        at = pl.ds(first, last - first)
        origin = adj_ref if slot == 0 else field
        return pltpu.make_async_remote_copy(
            src_ref=origin.at[pl.ds(1, 2), 0, at],
            dst_ref=from_high.at[slot, :, at],
            send_sem=send_down.at[slot, part],
            recv_sem=recv_high.at[slot, part],
            device_id=(grp, low),
            device_id_type=MESH,
        )

    def send_high(slot, part):
        x = cells - 1
        for y, size in pieces(*halves(slot)[part]):
            e0, e1, e2 = (field[a, x, pl.ds(y, size), :] for a in range(3))
            e0y = field[0, x, pl.ds(y + 1, size), :]
            to_high[slot, 0, pl.ds(y, size), :] = inv[x, pl.ds(y, size), :] * (next_z(e0) - e0) + e2
            to_high[slot, 1, pl.ds(y, size), :] = (e0 - e0y) - e1

        @pl.when(has_high)
        def _():
            copy_up(slot, part).start()

    def send_low(slot, part):
        @pl.when(has_low)
        def _():
            copy_down(slot, part).start()

    def curl_row(x, next_row, where=chunks):
        for y, size in where:
            at = pl.ds(y, size)
            e0, e1, e2 = (field[a, x, at, :] for a in range(3))
            e0y, e2y = field[0, x, pl.ds(y + 1, size), :], field[2, x, pl.ds(y + 1, size), :]
            e1x, e2x = next_row(at)
            h = inv[x, at, :]
            to = pl.ds(y + 8, size)
            curl[0, x + 1, to, :] = (e2y - e2) - h * (next_z(e1) - e1)
            curl[1, x + 1, to, :] = h * (next_z(e0) - e0) - (e2x - e2)
            curl[2, x + 1, to, :] = (e1x - e1) - (e0y - e0)

    def update_row(s, x, where=chunks):
        for y, size in where:
            at, to, before = pl.ds(y, size), pl.ds(y + 8, size), pl.ds(y + 7, size)
            h, c = inv[x, at, :], coef[x, at, :]
            h0, h1, h2 = (curl[a, x + 1, to, :] for a in range(3))
            h0y, h2y = curl[0, x + 1, before, :], curl[2, x + 1, before, :]
            h1x, h2x = curl[1, x, to, :], curl[2, x, to, :]
            image = (
                (h2 - h2y) - h * (h1 - last_z(h1)),
                h * (h0 - last_z(h0)) - (h2 - h2x),
                (h1 - h1x) - (h0 - h0y),
            )
            shift = nz - 1 - (2 + s) * cells - x
            source = pltpu.roll(columns[at, :], shift, 1)
            source = jnp.where(lane_index(source.shape) == nz - 1, source, 0.0)
            for a in range(3):
                value = field[a, x, at, :] - c * image[a]
                field[a, x, at, :] = value + source if a == 2 else value

    def product_row(s, x):
        for y, size in chunks:
            at = pl.ds(y, size)
            value = sum(field[a, x, at, :] * terms[s, a, x, at, :].astype(jnp.float32) for a in range(3))
            total[x, at, :] = value if s == 0 else total[x, at, :] + value

    pl.semaphore_wait(barrier, 2)
    send_low(0, 0)
    load_last.wait()
    send_high(0, 0)
    send_low(0, 1)
    send_high(0, 1)
    load_rest.wait()

    def model_up():
        return pltpu.make_async_remote_copy(
            src_ref=model_hbm.at[rows_v - 1],
            dst_ref=model_low,
            send_sem=model_send.at[0],
            recv_sem=model_recv.at[0],
            device_id=(grp, high),
            device_id_type=MESH,
        )

    def model_down():
        return pltpu.make_async_remote_copy(
            src_ref=model_hbm.at[0],
            dst_ref=model_high,
            send_sem=model_send.at[1],
            recv_sem=model_recv.at[1],
            device_id=(grp, low),
            device_id_type=MESH,
        )

    @pl.when(has_high)
    def _():
        model_up().start()

    @pl.when(has_low)
    def _():
        model_down().start()

    load_coef.wait()

    def coefficient_row(x, carry):
        coef[x] = 0.05 * jnp.exp(-0.7 * coef[x])
        return carry

    lax.fori_loop(0, cells, coefficient_row, 0)

    @pl.when(jnp.logical_not(has_low))
    def _():
        model_low[...] = jnp.zeros_like(model_low)

    @pl.when(jnp.logical_not(has_high))
    def _():
        model_high[...] = jnp.zeros_like(model_high)
        for s in range(steps):
            from_high[s] = jnp.zeros(from_high.shape[1:], jnp.float32)

    def regularize():
        @pl.when(has_high)
        def _():
            model_up().wait_send()
            model_down().wait_recv()

        @pl.when(has_low)
        def _():
            model_down().wait_send()
            model_up().wait_recv()

        small[3].wait()
        for v in range(rows_v):
            model[v, pl.ds(0, 8), :] = jnp.zeros((8, nz), jnp.float32)
            model[v, pl.ds(ny + 8, 8), :] = jnp.zeros((8, nz), jnp.float32)
            model[v, pl.ds(8, ny), :] = model_ref[v]
        for v in range(rows_v):
            for y, size in chunks:
                at = pl.ds(y, size)
                center = model_ref[v, at, :]
                below = model_low[at, :] if v == 0 else model_ref[v - 1, at, :]
                above = model_high[at, :] if v == rows_v - 1 else model_ref[v + 1, at, :]
                sides = model[v, pl.ds(y + 7, size), :] + model[v, pl.ds(y + 9, size), :]
                around = below + above + sides + next_z(center) + last_z(center)
                reg_ref[v, at, :] = 0.1 * (6.0 * center - around)

    def store(first, count, sem):
        return pltpu.make_async_copy(
            field.at[:, pl.ds(first, count), pl.ds(0, ny)], out_ref.at[:, pl.ds(first, count)], local_sem.at[sem]
        )

    def sensitivity_row(x, carry):
        product_row(steps - 1, x)
        limit = pltpu.roll(columns[...], nz - cells - x, 1)
        limit = jnp.broadcast_to(limit[:, 0:1], (ny, nz))
        inside = lane_index((ny, nz)).astype(jnp.float32) < limit
        sens = jnp.where(inside, -0.7 * coef[x] * total[x], 0.0)
        coarse = sens.astype(jnp.bfloat16)
        sens_ref[x, :, 0:nz] = coarse
        sens_ref[x, :, nz : 2 * nz] = (sens - coarse.astype(jnp.float32)).astype(jnp.bfloat16)
        return carry

    for s in range(steps):

        def inner_curl(x, carry):
            curl_row(x, lambda at: (field[1, x + 1, at, :], field[2, x + 1, at, :]))
            return carry

        lax.fori_loop(0, cells - 1, inner_curl, 0)
        if s > 0:

            def late_product(x, carry):
                product_row(s - 1, x)
                return carry

            load_terms[s - 1].wait()
            lax.fori_loop(0, cells, late_product, 0)

        def inner_update(x, carry):
            update_row(s, x)
            return carry

        lax.fori_loop(1, cells - 1, inner_update, 0)
        if s == steps - 1:
            store(1, cells - 2, 3).start()
        if s == min(1, steps - 1):
            regularize()

        if s == steps - 1:
            load_terms[s].wait()
            lax.fori_loop(1, cells - 1, sensitivity_row, 0)
        for part, (first, last) in enumerate(halves(s)):
            where = pieces(first, last)

            @pl.when(has_high)
            def _():
                copy_up(s, part).wait_send()
                copy_down(s, part).wait_recv()

            curl_row(cells - 1, lambda at: (from_high[s, 0, at, :], from_high[s, 1, at, :]), where)
            update_row(s, cells - 1, where)
            if s < steps - 1:
                send_high(s + 1, part)

            @pl.when(has_low)
            def _():
                copy_down(s, part).wait_send()
                copy_up(s, part).wait_recv()
                for y, size in where:
                    at, to = pl.ds(y, size), pl.ds(y + 8, size)
                    curl[1, 0, to, :] = from_low[s, 0, at, :] - field[2, 0, at, :]
                    curl[2, 0, to, :] = from_low[s, 1, at, :] + field[1, 0, at, :]

            @pl.when(jnp.logical_not(has_low))
            def _():
                for a in (1, 2):
                    curl[a, 0, pl.ds(first + 8, last - first), :] = jnp.zeros((last - first, nz), jnp.float32)

            update_row(s, 0, where)
            if s < steps - 1:
                send_low(s + 1, part)
    store(0, 1, 4).start()
    store(cells - 1, 1, 5).start()

    sensitivity_row(0, 0)
    sensitivity_row(cells - 1, 0)
    store(1, cells - 2, 3).wait()
    store(0, 1, 4).wait()
    store(cells - 1, 1, 5).wait()


def field_phase(n, adj, fwd, logc, spacing, residuals, gates, counts, model):
    steps = fwd.shape[0]
    cells, ny, nz = logc.shape
    f32 = jnp.float32
    anywhere, far, vmem = pl.BlockSpec(memory_space=pl.ANY), pl.BlockSpec(memory_space=pltpu.HBM), pl.BlockSpec(memory_space=pltpu.VMEM)
    dma = pltpu.SemaphoreType.DMA
    return pl.pallas_call(
        functools.partial(field_kernel, n),
        out_shape=(
            jax.ShapeDtypeStruct(adj.shape, f32),
            jax.ShapeDtypeStruct((cells, ny, 2 * nz), jnp.bfloat16),
            jax.ShapeDtypeStruct(model.shape, f32),
        ),
        in_specs=[far] * 5 + [pl.BlockSpec(memory_space=pltpu.SMEM), far, far],
        out_specs=(anywhere, vmem, vmem),
        scratch_shapes=[
            pltpu.VMEM(spacing.shape, f32),
            pltpu.VMEM(residuals.shape, f32),
            pltpu.VMEM(counts.shape, jnp.int32),
            pltpu.VMEM(model.shape, f32),
            pltpu.VMEM((3, cells, ny + 8, nz), f32),
            pltpu.VMEM((3, cells + 1, ny + 8, nz), f32),
            pltpu.VMEM((cells, ny, nz), f32),
            pltpu.VMEM((cells, ny, nz), f32),
            pltpu.VMEM((cells, ny, nz), f32),
            pltpu.VMEM(fwd.shape, jnp.bfloat16),
            pltpu.VMEM((ny, nz), f32),
            pltpu.VMEM((steps, 2, ny, nz), f32),
            pltpu.VMEM((steps, 2, ny, nz), f32),
            pltpu.VMEM((steps, 2, ny, nz), f32),
            pltpu.VMEM((model.shape[0], ny + 16, nz), f32),
            pltpu.VMEM((ny, nz), f32),
            pltpu.VMEM((ny, nz), f32),
            dma((10,)),
            dma((steps,)),
            dma((steps, 2)),
            dma((steps, 2)),
            dma((steps, 2)),
            dma((steps, 2)),
            dma((2,)),
            dma((2,)),
        ],
        compiler_params=pltpu.CompilerParams(collective_id=0, has_side_effects=True, vmem_limit_bytes=60 << 20),
    )(adj, fwd, logc, spacing, residuals, gates, counts, model)


def relayout_kernel(
    n,
    sens_hbm,
    voxel_hbm,
    reg_hbm,
    out_ref,
    sens,
    voxel,
    ids,
    reg,
    to_pair,
    from_pair,
    across,
    from_across,
    held,
    arrived,
    load_sem,
    pair_send,
    pair_recv,
    across_send,
    across_recv,
    layer_send,
    layer_recv,
):
    layers = n // 4
    cells, ny = voxel_hbm.shape
    voxels, nz = reg_hbm.shape
    blocks, size = 2 * layers, voxels // 2
    grp, me = lax.axis_index("grp"), lax.axis_index("tx")
    core, half, layer = lax.rem(me, 2), lax.rem(me // 2, 2), me // 4
    up = jnp.where(layer < layers // 2, 1, 0)

    def tile(z, y, c):
        return (z * 2 + y) * 2 + c

    def layer_at(k):
        return up * (layers - 1 - k) + (1 - up) * k

    loads = [
        pltpu.make_async_copy(source, target, load_sem.at[i])
        for i, (source, target) in enumerate(((sens_hbm, sens), (voxel_hbm, voxel), (reg_hbm, reg)))
    ]
    for copy in loads:
        copy.start()
    barrier = pltpu.get_barrier_semaphore()
    for other in (tile(layer, half, 1 - core), tile(layer, 1 - half, core)):
        pl.semaphore_signal(barrier, inc=1, device_id=(grp, other), device_id_type=MESH)

    def greet(z, carry):
        @pl.when(z != layer)
        def _():
            pl.semaphore_signal(
                barrier, inc=1, device_id=(grp, tile(z, half, core)), device_id_type=MESH
            )

        return carry

    lax.fori_loop(0, layers, greet, 0)
    for copy in loads:
        copy.wait()
    for x in range(cells):
        ids[:, x * ny : (x + 1) * ny] = voxel[x : x + 1, :]

    def pair_copy(k, y):
        return pltpu.make_async_remote_copy(
            src_ref=to_pair.at[k, y],
            dst_ref=from_pair.at[k, y],
            send_sem=pair_send.at[k, y],
            recv_sem=pair_recv.at[k, y],
            device_id=(grp, tile(layer, half, 1 - core)),
            device_id_type=MESH,
        )

    def across_copy(k):
        return pltpu.make_async_remote_copy(
            src_ref=across.at[k],
            dst_ref=from_across.at[k],
            send_sem=across_send.at[k],
            recv_sem=across_recv.at[k],
            device_id=(grp, tile(layer, 1 - half, core)),
            device_id_type=MESH,
        )

    def layer_copy(k):
        return pltpu.make_async_remote_copy(
            src_ref=held.at[k],
            dst_ref=arrived.at[layer, lax.rem(k, 2)],
            send_sem=layer_send.at[k],
            recv_sem=layer_recv.at[layer, lax.rem(k, 2)],
            device_id=(grp, tile(layer_at(k // 2), half, core)),
            device_id_type=MESH,
        )

    def arrival(z, part):
        return pltpu.make_async_remote_copy(
            src_ref=held.at[0],
            dst_ref=arrived.at[z, part],
            send_sem=layer_send.at[0],
            recv_sem=layer_recv.at[z, part],
            device_id=(grp, tile(z, half, core)),
            device_id_type=MESH,
        )

    def target_sums(k, y, c):
        first = tile(layer_at(k // 2), y, c) * voxels + lax.rem(k, 2) * size
        here = lax.broadcasted_iota(jnp.int32, (size, cells * ny), 0) == ids[...] - first
        picked = jnp.where(here, 1.0, 0.0).astype(jnp.bfloat16)
        sums = jnp.dot(picked, sens[...], preferred_element_type=jnp.float32)
        return sums[:, 0:nz] + sums[:, nz : 2 * nz]

    def forward(k):
        across_copy(k).wait_recv()
        pair_copy(k, 1).wait_recv()
        held[k] = held[k] + from_pair[k, 1] + from_across[k]

        @pl.when(layer_at(k // 2) != layer)
        def _():
            layer_copy(k).start()

    def stage(k, carry):
        across[k] = target_sums(k, 1 - half, core)
        pair_copy(k, 0).wait_recv()
        across[k] = across[k] + from_pair[k, 0]
        across_copy(k).start()

        @pl.when(k < blocks - 1)
        def _():
            to_pair[k + 1, 0] = target_sums(k + 1, 1 - half, 1 - core)
            pair_copy(k + 1, 0).start()

        to_pair[k, 1] = target_sums(k, half, 1 - core)
        pair_copy(k, 1).start()
        held[k] = target_sums(k, half, core)

        @pl.when(k > 0)
        def _():
            forward(k - 1)

        return carry

    to_pair[0, 0] = target_sums(0, 1 - half, 1 - core)
    pl.semaphore_wait(barrier, layers + 1)
    pair_copy(0, 0).start()
    lax.fori_loop(0, blocks, stage, 0)
    forward(blocks - 1)
    own = up * (layers - 1 - layer) + (1 - up) * layer
    for part in range(2):
        at = pl.ds(part * size, size)
        out_ref[at, :] = reg[at, :] + held[2 * own + part]

    def collect(z, carry):
        @pl.when(z != layer)
        def _():
            for part in range(2):
                at = pl.ds(part * size, size)
                arrival(z, part).wait_recv()
                out_ref[at, :] = out_ref[at, :] + arrived[z, part]

        return carry

    lax.fori_loop(0, layers, collect, 0)

    def drain(k, carry):
        pair_copy(k, 0).wait_send()
        pair_copy(k, 1).wait_send()
        across_copy(k).wait_send()

        @pl.when(layer_at(k // 2) != layer)
        def _():
            layer_copy(k).wait_send()

        return carry

    lax.fori_loop(0, blocks, drain, 0)


def relayout(n, sensitivity, voxel_column, regularity):
    cells, ny = voxel_column.shape
    nz = regularity.shape[2]
    voxels = regularity.shape[0] * regularity.shape[1]
    layers = n // 4
    f32, dma = jnp.float32, pltpu.SemaphoreType.DMA
    far = pl.BlockSpec(memory_space=pltpu.HBM)
    block, part = (voxels, nz), (voxels // 2, nz)
    blocks = 2 * layers
    out = pl.pallas_call(
        functools.partial(relayout_kernel, n),
        out_shape=jax.ShapeDtypeStruct(block, f32),
        in_specs=[far] * 3,
        out_specs=pl.BlockSpec(memory_space=pltpu.VMEM),
        scratch_shapes=[
            pltpu.VMEM((cells * ny, 2 * nz), jnp.bfloat16),
            pltpu.VMEM((cells, ny), jnp.int32),
            pltpu.VMEM((1, cells * ny), jnp.int32),
            pltpu.VMEM(block, f32),
            pltpu.VMEM((blocks, 2) + part, f32),
            pltpu.VMEM((blocks, 2) + part, f32),
            pltpu.VMEM((blocks,) + part, f32),
            pltpu.VMEM((blocks,) + part, f32),
            pltpu.VMEM((blocks,) + part, f32),
            pltpu.VMEM((layers, 2) + part, f32),
            dma((3,)),
            dma((blocks, 2)),
            dma((blocks, 2)),
            dma((blocks,)),
            dma((blocks,)),
            dma((blocks,)),
            dma((layers, 2)),
        ],
        compiler_params=pltpu.CompilerParams(collective_id=1, has_side_effects=True, vmem_limit_bytes=60 << 20),
    )(sensitivity.reshape(cells * ny, 2 * nz), voxel_column, regularity.reshape(block))
    return out.reshape(regularity.shape)


def deliver_kernel(adj_ref, grad_ref, adj_out, grad_out, adj, grad, load_sem, store_sem):
    cells = adj_ref.shape[1]
    moves = [(adj_ref.at[:, x], adj.at[:, x], adj_out.at[:, x]) for x in range(cells)]
    moves.append((grad_ref, grad, grad_out))
    loads = [pltpu.make_async_copy(a, b, load_sem.at[i]) for i, (a, b, _) in enumerate(moves)]
    stores = [pltpu.make_async_copy(b, c, store_sem.at[i]) for i, (_, b, c) in enumerate(moves)]
    for copy in loads:
        copy.start()
    for load, copy in zip(loads, stores):
        load.wait()
        copy.start()
    for copy in stores:
        copy.wait()


def deliver(adjoint, gradient):
    far = pl.BlockSpec(memory_space=pltpu.HBM)
    copies = adjoint.shape[1] + 1
    return pl.pallas_call(
        deliver_kernel,
        out_shape=tuple(jax.ShapeDtypeStruct(v.shape, v.dtype) for v in (adjoint, gradient)),
        in_specs=[far, far],
        out_specs=(far, far),
        scratch_shapes=[
            pltpu.VMEM(adjoint.shape, adjoint.dtype),
            pltpu.VMEM(gradient.shape, gradient.dtype),
            pltpu.SemaphoreType.DMA((copies,)),
            pltpu.SemaphoreType.DMA((copies,)),
        ],
        compiler_params=pltpu.CompilerParams(vmem_limit_bytes=60 << 20),
    )(adjoint, gradient)


def body(
    adjoint_in,
    forward_terms,
    log_conductivity,
    spacing,
    residuals,
    gate_index,
    counts,
    voxel_column,
    voxel_model,
):
    tile_count = lax.axis_size("tx")
    adjoint, sensitivity, regularity = field_phase(
        tile_count,
        adjoint_in,
        forward_terms,
        log_conductivity,
        spacing,
        residuals,
        gate_index,
        counts,
        voxel_model,
    )
    gradient = relayout(tile_count, sensitivity, voxel_column, regularity)
    return deliver(adjoint, gradient)


def solution(mesh):
    in_specs = (
        P(None, ("grp", "tx"), None, None),
        P(None, None, ("grp", "tx"), None, None),
        P(("grp", "tx"), None, None),
        P(("grp", "tx"), None),
        P(None, ("grp", "tx"), None),
        P("grp"),
        P(("grp", "tx"), None),
        P(("grp", "tx"), None),
        P(("grp", "tx"), None, None),
    )
    out_specs = (P(None, ("grp", "tx"), None, None), P(("grp", "tx"), None, None))
    return jax.shard_map(body, mesh=mesh, in_specs=in_specs, out_specs=out_specs, check_vma=False)
```

```python
import functools

import jax
import jax.numpy as jnp
from jax import lax
from jax.experimental import pallas as pl
from jax.experimental.pallas import tpu as pltpu
from jax.sharding import PartitionSpec as P

MESH = pl.DeviceIdType.MESH


def lane_index(shape):
    return lax.broadcasted_iota(jnp.int32, shape, 1)


def next_z(value):
    depth = value.shape[1]
    return jnp.where(lane_index(value.shape) < depth - 1, pltpu.roll(value, depth - 1, 1), 0.0)


def last_z(value):
    return jnp.where(lane_index(value.shape) > 0, pltpu.roll(value, 1, 1), 0.0)


def field_kernel(
    n,
    adj_ref,
    fwd_ref,
    logc_ref,
    spacing_hbm,
    residual_hbm,
    gate_ref,
    counts_hbm,
    model_hbm,
    out_ref,
    sens_ref,
    reg_ref,
    spacing_ref,
    residual_ref,
    counts_ref,
    model_ref,
    field,
    curl,
    coef,
    inv,
    total,
    terms,
    columns,
    from_low,
    from_high,
    to_high,
    model,
    model_low,
    model_high,
    local_sem,
    term_sem,
    send_up,
    send_down,
    recv_low,
    recv_high,
    model_send,
    model_recv,
):
    steps = fwd_ref.shape[0]
    cells, ny, nz = logc_ref.shape
    rows_v = model_hbm.shape[0]
    grp, me = lax.axis_index("grp"), lax.axis_index("tx")
    low, high = lax.rem(me + n - 1, n), lax.rem(me + 1, n)
    has_low, has_high = me > 0, me < n - 1
    chunk = 64


    def pieces(first, last):
        return [(y, min(chunk, last - y)) for y in range(first, last, chunk)]

    chunks = pieces(0, ny)

    def halves(slot):
        middle = ny // 2 + 8 * (1 - slot)
        return ((0, middle), (middle, ny))

    small = [
        pltpu.make_async_copy(source, target, local_sem.at[6 + i])
        for i, (source, target) in enumerate(
            (
                (spacing_hbm, spacing_ref),
                (counts_hbm, counts_ref),
                (residual_hbm, residual_ref),
                (model_hbm, model_ref),
            )
        )
    ]
    for copy in small[:3]:
        copy.start()
    load_last = pltpu.make_async_copy(
        adj_ref.at[:, pl.ds(cells - 1, 1)], field.at[:, pl.ds(cells - 1, 1), pl.ds(0, ny)], local_sem.at[0]
    )
    load_last.start()
    load_rest = pltpu.make_async_copy(
        adj_ref.at[:, pl.ds(0, cells - 1)], field.at[:, pl.ds(0, cells - 1), pl.ds(0, ny)], local_sem.at[1]
    )
    load_rest.start()
    load_coef = pltpu.make_async_copy(logc_ref, coef, local_sem.at[2])
    load_coef.start()
    load_terms = [pltpu.make_async_copy(fwd_ref.at[s], terms.at[s], term_sem.at[s]) for s in range(steps)]
    for copy in load_terms:
        copy.start()
    small[3].start()

    barrier = pltpu.get_barrier_semaphore()
    for neighbour in (low, high):
        pl.semaphore_signal(barrier, inc=1, device_id=(grp, neighbour), device_id_type=MESH)

    for copy in small[:3]:
        copy.wait()
    inverse = 1.0 / spacing_ref[...]
    depth_count = counts_ref[...].astype(jnp.float32)
    sources = [residual_ref[gate_ref[s]] for s in range(steps)]
    for y in range(0, ny, nz):
        parts = [v[:, y : y + nz] for v in [inverse, depth_count] + sources]
        parts.append(jnp.zeros((nz - cells * (2 + steps), nz), jnp.float32))
        columns[pl.ds(y, nz), :] = jnp.concatenate(parts, axis=0).T

    for x in range(cells):
        inv[x] = jnp.broadcast_to(columns[:, x : x + 1], (ny, nz))
        for a in range(3):
            field[a, x, pl.ds(ny, 8), :] = jnp.zeros((8, nz), jnp.float32)
            curl[a, x + 1, pl.ds(0, 8), :] = jnp.zeros((8, nz), jnp.float32)

    def copy_up(slot, part):
        first, last = halves(slot)[part]
        at = pl.ds(first, last - first)
        return pltpu.make_async_remote_copy(
            src_ref=to_high.at[slot, :, at],
            dst_ref=from_low.at[slot, :, at],
            send_sem=send_up.at[slot, part],
            recv_sem=recv_low.at[slot, part],
            device_id=(grp, high),
            device_id_type=MESH,
        )

    def copy_down(slot, part):
        first, last = halves(slot)[part]
        at = pl.ds(first, last - first)
        origin = adj_ref if slot == 0 else field
        return pltpu.make_async_remote_copy(
            src_ref=origin.at[pl.ds(1, 2), 0, at],
            dst_ref=from_high.at[slot, :, at],
            send_sem=send_down.at[slot, part],
            recv_sem=recv_high.at[slot, part],
            device_id=(grp, low),
            device_id_type=MESH,
        )

    def send_high(slot, part):
        x = cells - 1
        for y, size in pieces(*halves(slot)[part]):
            e0, e1, e2 = (field[a, x, pl.ds(y, size), :] for a in range(3))
            e0y = field[0, x, pl.ds(y + 1, size), :]
            to_high[slot, 0, pl.ds(y, size), :] = inv[x, pl.ds(y, size), :] * (next_z(e0) - e0) + e2
            to_high[slot, 1, pl.ds(y, size), :] = (e0 - e0y) - e1

        @pl.when(has_high)
        def _():
            copy_up(slot, part).start()

    def send_low(slot, part):
        @pl.when(has_low)
        def _():
            copy_down(slot, part).start()

    def curl_row(x, next_row, where=chunks):
        for y, size in where:
            at = pl.ds(y, size)
            e0, e1, e2 = (field[a, x, at, :] for a in range(3))
            e0y, e2y = field[0, x, pl.ds(y + 1, size), :], field[2, x, pl.ds(y + 1, size), :]
            e1x, e2x = next_row(at)
            h = inv[x, at, :]
            to = pl.ds(y + 8, size)
            curl[0, x + 1, to, :] = (e2y - e2) - h * (next_z(e1) - e1)
            curl[1, x + 1, to, :] = h * (next_z(e0) - e0) - (e2x - e2)
            curl[2, x + 1, to, :] = (e1x - e1) - (e0y - e0)

    def update_row(s, x, where=chunks):
        for y, size in where:
            at, to, before = pl.ds(y, size), pl.ds(y + 8, size), pl.ds(y + 7, size)
            h, c = inv[x, at, :], coef[x, at, :]
            h0, h1, h2 = (curl[a, x + 1, to, :] for a in range(3))
            h0y, h2y = curl[0, x + 1, before, :], curl[2, x + 1, before, :]
            h1x, h2x = curl[1, x, to, :], curl[2, x, to, :]
            image = (
                (h2 - h2y) - h * (h1 - last_z(h1)),
                h * (h0 - last_z(h0)) - (h2 - h2x),
                (h1 - h1x) - (h0 - h0y),
            )
            shift = nz - 1 - (2 + s) * cells - x
            source = pltpu.roll(columns[at, :], shift, 1)
            source = jnp.where(lane_index(source.shape) == nz - 1, source, 0.0)
            for a in range(3):
                value = field[a, x, at, :] - c * image[a]
                field[a, x, at, :] = value + source if a == 2 else value

    def product_row(s, x):
        for y, size in chunks:
            at = pl.ds(y, size)
            value = sum(field[a, x, at, :] * terms[s, a, x, at, :].astype(jnp.float32) for a in range(3))
            total[x, at, :] = value if s == 0 else total[x, at, :] + value

    pl.semaphore_wait(barrier, 2)
    send_low(0, 0)
    load_last.wait()
    send_high(0, 0)
    send_low(0, 1)
    send_high(0, 1)
    load_rest.wait()

    def model_up():
        return pltpu.make_async_remote_copy(
            src_ref=model_hbm.at[rows_v - 1],
            dst_ref=model_low,
            send_sem=model_send.at[0],
            recv_sem=model_recv.at[0],
            device_id=(grp, high),
            device_id_type=MESH,
        )

    def model_down():
        return pltpu.make_async_remote_copy(
            src_ref=model_hbm.at[0],
            dst_ref=model_high,
            send_sem=model_send.at[1],
            recv_sem=model_recv.at[1],
            device_id=(grp, low),
            device_id_type=MESH,
        )

    @pl.when(has_high)
    def _():
        model_up().start()

    @pl.when(has_low)
    def _():
        model_down().start()

    load_coef.wait()

    def coefficient_row(x, carry):
        coef[x] = 0.05 * jnp.exp(-0.7 * coef[x])
        return carry

    lax.fori_loop(0, cells, coefficient_row, 0)

    @pl.when(jnp.logical_not(has_low))
    def _():
        model_low[...] = jnp.zeros_like(model_low)

    @pl.when(jnp.logical_not(has_high))
    def _():
        model_high[...] = jnp.zeros_like(model_high)
        for s in range(steps):
            from_high[s] = jnp.zeros(from_high.shape[1:], jnp.float32)

    def regularize():
        @pl.when(has_high)
        def _():
            model_up().wait_send()
            model_down().wait_recv()

        @pl.when(has_low)
        def _():
            model_down().wait_send()
            model_up().wait_recv()

        small[3].wait()
        for v in range(rows_v):
            model[v, pl.ds(0, 8), :] = jnp.zeros((8, nz), jnp.float32)
            model[v, pl.ds(ny + 8, 8), :] = jnp.zeros((8, nz), jnp.float32)
            model[v, pl.ds(8, ny), :] = model_ref[v]
        for v in range(rows_v):
            for y, size in chunks:
                at = pl.ds(y, size)
                center = model_ref[v, at, :]
                below = model_low[at, :] if v == 0 else model_ref[v - 1, at, :]
                above = model_high[at, :] if v == rows_v - 1 else model_ref[v + 1, at, :]
                sides = model[v, pl.ds(y + 7, size), :] + model[v, pl.ds(y + 9, size), :]
                around = below + above + sides + next_z(center) + last_z(center)
                reg_ref[v, at, :] = 0.1 * (6.0 * center - around)

    def store(first, count, sem):
        return pltpu.make_async_copy(
            field.at[:, pl.ds(first, count), pl.ds(0, ny)], out_ref.at[:, pl.ds(first, count)], local_sem.at[sem]
        )

    def sensitivity_row(x, carry):
        product_row(steps - 1, x)
        limit = pltpu.roll(columns[...], nz - cells - x, 1)
        limit = jnp.broadcast_to(limit[:, 0:1], (ny, nz))
        inside = lane_index((ny, nz)).astype(jnp.float32) < limit
        sens = jnp.where(inside, -0.7 * coef[x] * total[x], 0.0)
        coarse = sens.astype(jnp.bfloat16)
        sens_ref[x, :, 0:nz] = coarse
        sens_ref[x, :, nz : 2 * nz] = (sens - coarse.astype(jnp.float32)).astype(jnp.bfloat16)
        return carry

    for s in range(steps):

        def inner_curl(x, carry):
            curl_row(x, lambda at: (field[1, x + 1, at, :], field[2, x + 1, at, :]))
            return carry

        lax.fori_loop(0, cells - 1, inner_curl, 0)
        if s > 0:

            def late_product(x, carry):
                product_row(s - 1, x)
                return carry

            load_terms[s - 1].wait()
            lax.fori_loop(0, cells, late_product, 0)

        def inner_update(x, carry):
            update_row(s, x)
            return carry

        lax.fori_loop(1, cells - 1, inner_update, 0)
        if s == steps - 1:
            store(1, cells - 2, 3).start()
        if s == min(1, steps - 1):
            regularize()

        if s == steps - 1:
            load_terms[s].wait()
            lax.fori_loop(1, cells - 1, sensitivity_row, 0)
        for part, (first, last) in enumerate(halves(s)):
            where = pieces(first, last)

            @pl.when(has_high)
            def _():
                copy_up(s, part).wait_send()
                copy_down(s, part).wait_recv()

            curl_row(cells - 1, lambda at: (from_high[s, 0, at, :], from_high[s, 1, at, :]), where)
            update_row(s, cells - 1, where)
            if s < steps - 1:
                send_high(s + 1, part)

            @pl.when(has_low)
            def _():
                copy_down(s, part).wait_send()
                copy_up(s, part).wait_recv()
                for y, size in where:
                    at, to = pl.ds(y, size), pl.ds(y + 8, size)
                    curl[1, 0, to, :] = from_low[s, 0, at, :] - field[2, 0, at, :]
                    curl[2, 0, to, :] = from_low[s, 1, at, :] + field[1, 0, at, :]

            @pl.when(jnp.logical_not(has_low))
            def _():
                for a in (1, 2):
                    curl[a, 0, pl.ds(first + 8, last - first), :] = jnp.zeros((last - first, nz), jnp.float32)

            update_row(s, 0, where)
            if s < steps - 1:
                send_low(s + 1, part)
    store(0, 1, 4).start()
    store(cells - 1, 1, 5).start()

    sensitivity_row(0, 0)
    sensitivity_row(cells - 1, 0)
    store(1, cells - 2, 3).wait()
    store(0, 1, 4).wait()
    store(cells - 1, 1, 5).wait()


def field_phase(n, adj, fwd, logc, spacing, residuals, gates, counts, model):
    steps = fwd.shape[0]
    cells, ny, nz = logc.shape
    f32 = jnp.float32
    anywhere, far, vmem = pl.BlockSpec(memory_space=pl.ANY), pl.BlockSpec(memory_space=pltpu.HBM), pl.BlockSpec(memory_space=pltpu.VMEM)
    dma = pltpu.SemaphoreType.DMA
    return pl.pallas_call(
        functools.partial(field_kernel, n),
        out_shape=(
            jax.ShapeDtypeStruct(adj.shape, f32),
            jax.ShapeDtypeStruct((cells, ny, 2 * nz), jnp.bfloat16),
            jax.ShapeDtypeStruct(model.shape, f32),
        ),
        in_specs=[far] * 5 + [pl.BlockSpec(memory_space=pltpu.SMEM), far, far],
        out_specs=(anywhere, vmem, vmem),
        scratch_shapes=[
            pltpu.VMEM(spacing.shape, f32),
            pltpu.VMEM(residuals.shape, f32),
            pltpu.VMEM(counts.shape, jnp.int32),
            pltpu.VMEM(model.shape, f32),
            pltpu.VMEM((3, cells, ny + 8, nz), f32),
            pltpu.VMEM((3, cells + 1, ny + 8, nz), f32),
            pltpu.VMEM((cells, ny, nz), f32),
            pltpu.VMEM((cells, ny, nz), f32),
            pltpu.VMEM((cells, ny, nz), f32),
            pltpu.VMEM(fwd.shape, jnp.bfloat16),
            pltpu.VMEM((ny, nz), f32),
            pltpu.VMEM((steps, 2, ny, nz), f32),
            pltpu.VMEM((steps, 2, ny, nz), f32),
            pltpu.VMEM((steps, 2, ny, nz), f32),
            pltpu.VMEM((model.shape[0], ny + 16, nz), f32),
            pltpu.VMEM((ny, nz), f32),
            pltpu.VMEM((ny, nz), f32),
            dma((10,)),
            dma((steps,)),
            dma((steps, 2)),
            dma((steps, 2)),
            dma((steps, 2)),
            dma((steps, 2)),
            dma((2,)),
            dma((2,)),
        ],
        compiler_params=pltpu.CompilerParams(collective_id=0, has_side_effects=True, vmem_limit_bytes=60 << 20),
    )(adj, fwd, logc, spacing, residuals, gates, counts, model)


def relayout_kernel(
    n,
    sens_hbm,
    voxel_hbm,
    reg_hbm,
    out_ref,
    sens,
    voxel,
    ids,
    reg,
    to_pair,
    from_pair,
    across,
    from_across,
    held,
    arrived,
    load_sem,
    pair_send,
    pair_recv,
    across_send,
    across_recv,
    layer_send,
    layer_recv,
):
    layers = n // 4
    cells, ny = voxel_hbm.shape
    voxels, nz = reg_hbm.shape
    blocks, size = 2 * layers, voxels // 2
    grp, me = lax.axis_index("grp"), lax.axis_index("tx")
    core, half, layer = lax.rem(me, 2), lax.rem(me // 2, 2), me // 4
    up = jnp.where(layer < layers // 2, 1, 0)

    def tile(z, y, c):
        return (z * 2 + y) * 2 + c

    def layer_at(k):
        above = layers - 1 - layer
        rising = jnp.where(k < above, layers - 1 - k, k - above)
        falling = jnp.where(k < layer, k, layers - 1 - (k - layer))
        return up * rising + (1 - up) * falling

    loads = [
        pltpu.make_async_copy(source, target, load_sem.at[i])
        for i, (source, target) in enumerate(((sens_hbm, sens), (voxel_hbm, voxel), (reg_hbm, reg)))
    ]
    for copy in loads:
        copy.start()
    barrier = pltpu.get_barrier_semaphore()
    for other in (tile(layer, half, 1 - core), tile(layer, 1 - half, core)):
        pl.semaphore_signal(barrier, inc=1, device_id=(grp, other), device_id_type=MESH)

    def greet(z, carry):
        @pl.when(z != layer)
        def _():
            pl.semaphore_signal(
                barrier, inc=1, device_id=(grp, tile(z, half, core)), device_id_type=MESH
            )

        return carry

    lax.fori_loop(0, layers, greet, 0)
    for copy in loads:
        copy.wait()
    for x in range(cells):
        ids[:, x * ny : (x + 1) * ny] = voxel[x : x + 1, :]

    def pair_copy(k, y):
        return pltpu.make_async_remote_copy(
            src_ref=to_pair.at[k, y],
            dst_ref=from_pair.at[k, y],
            send_sem=pair_send.at[k, y],
            recv_sem=pair_recv.at[k, y],
            device_id=(grp, tile(layer, half, 1 - core)),
            device_id_type=MESH,
        )

    def across_copy(k):
        return pltpu.make_async_remote_copy(
            src_ref=across.at[k],
            dst_ref=from_across.at[k],
            send_sem=across_send.at[k],
            recv_sem=across_recv.at[k],
            device_id=(grp, tile(layer, 1 - half, core)),
            device_id_type=MESH,
        )

    def layer_copy(k):
        return pltpu.make_async_remote_copy(
            src_ref=held.at[k],
            dst_ref=arrived.at[layer, lax.rem(k, 2)],
            send_sem=layer_send.at[k],
            recv_sem=layer_recv.at[layer, lax.rem(k, 2)],
            device_id=(grp, tile(layer_at(k // 2), half, core)),
            device_id_type=MESH,
        )

    def arrival(z, part):
        return pltpu.make_async_remote_copy(
            src_ref=held.at[0],
            dst_ref=arrived.at[z, part],
            send_sem=layer_send.at[0],
            recv_sem=layer_recv.at[z, part],
            device_id=(grp, tile(z, half, core)),
            device_id_type=MESH,
        )

    def target_sums(k, y, c):
        first = tile(layer_at(k // 2), y, c) * voxels + lax.rem(k, 2) * size
        here = lax.broadcasted_iota(jnp.int32, (size, cells * ny), 0) == ids[...] - first
        picked = jnp.where(here, 1.0, 0.0).astype(jnp.bfloat16)
        sums = jnp.dot(picked, sens[...], preferred_element_type=jnp.float32)
        return sums[:, 0:nz] + sums[:, nz : 2 * nz]

    def forward(k):
        across_copy(k).wait_recv()
        pair_copy(k, 1).wait_recv()
        held[k] = held[k] + from_pair[k, 1] + from_across[k]

        @pl.when(layer_at(k // 2) != layer)
        def _():
            layer_copy(k).start()

    def stage(k, carry):
        across[k] = target_sums(k, 1 - half, core)
        pair_copy(k, 0).wait_recv()
        across[k] = across[k] + from_pair[k, 0]
        across_copy(k).start()

        @pl.when(k < blocks - 1)
        def _():
            to_pair[k + 1, 0] = target_sums(k + 1, 1 - half, 1 - core)
            pair_copy(k + 1, 0).start()

        to_pair[k, 1] = target_sums(k, half, 1 - core)
        pair_copy(k, 1).start()
        held[k] = target_sums(k, half, core)

        @pl.when(k > 0)
        def _():
            forward(k - 1)

        return carry

    to_pair[0, 0] = target_sums(0, 1 - half, 1 - core)
    pl.semaphore_wait(barrier, layers + 1)
    pair_copy(0, 0).start()
    lax.fori_loop(0, blocks, stage, 0)
    forward(blocks - 1)
    own = layers - 1
    for part in range(2):
        at = pl.ds(part * size, size)
        out_ref[at, :] = reg[at, :] + held[2 * own + part]

    def collect(z, carry):
        @pl.when(z != layer)
        def _():
            for part in range(2):
                at = pl.ds(part * size, size)
                arrival(z, part).wait_recv()
                out_ref[at, :] = out_ref[at, :] + arrived[z, part]

        return carry

    lax.fori_loop(0, layers, collect, 0)

    def drain(k, carry):
        pair_copy(k, 0).wait_send()
        pair_copy(k, 1).wait_send()
        across_copy(k).wait_send()

        @pl.when(layer_at(k // 2) != layer)
        def _():
            layer_copy(k).wait_send()

        return carry

    lax.fori_loop(0, blocks, drain, 0)


def relayout(n, sensitivity, voxel_column, regularity):
    cells, ny = voxel_column.shape
    nz = regularity.shape[2]
    voxels = regularity.shape[0] * regularity.shape[1]
    layers = n // 4
    f32, dma = jnp.float32, pltpu.SemaphoreType.DMA
    far = pl.BlockSpec(memory_space=pltpu.HBM)
    block, part = (voxels, nz), (voxels // 2, nz)
    blocks = 2 * layers
    out = pl.pallas_call(
        functools.partial(relayout_kernel, n),
        out_shape=jax.ShapeDtypeStruct(block, f32),
        in_specs=[far] * 3,
        out_specs=pl.BlockSpec(memory_space=pltpu.VMEM),
        scratch_shapes=[
            pltpu.VMEM((cells * ny, 2 * nz), jnp.bfloat16),
            pltpu.VMEM((cells, ny), jnp.int32),
            pltpu.VMEM((1, cells * ny), jnp.int32),
            pltpu.VMEM(block, f32),
            pltpu.VMEM((blocks, 2) + part, f32),
            pltpu.VMEM((blocks, 2) + part, f32),
            pltpu.VMEM((blocks,) + part, f32),
            pltpu.VMEM((blocks,) + part, f32),
            pltpu.VMEM((blocks,) + part, f32),
            pltpu.VMEM((layers, 2) + part, f32),
            dma((3,)),
            dma((blocks, 2)),
            dma((blocks, 2)),
            dma((blocks,)),
            dma((blocks,)),
            dma((blocks,)),
            dma((layers, 2)),
        ],
        compiler_params=pltpu.CompilerParams(collective_id=1, has_side_effects=True, vmem_limit_bytes=60 << 20),
    )(sensitivity.reshape(cells * ny, 2 * nz), voxel_column, regularity.reshape(block))
    return out.reshape(regularity.shape)


def deliver_kernel(adj_ref, grad_ref, adj_out, grad_out, adj, grad, load_sem, store_sem):
    cells = adj_ref.shape[1]
    moves = [(adj_ref.at[:, x], adj.at[:, x], adj_out.at[:, x]) for x in range(cells)]
    moves.append((grad_ref, grad, grad_out))
    loads = [pltpu.make_async_copy(a, b, load_sem.at[i]) for i, (a, b, _) in enumerate(moves)]
    stores = [pltpu.make_async_copy(b, c, store_sem.at[i]) for i, (_, b, c) in enumerate(moves)]
    for copy in loads:
        copy.start()
    for load, copy in zip(loads, stores):
        load.wait()
        copy.start()
    for copy in stores:
        copy.wait()


def deliver(adjoint, gradient):
    far = pl.BlockSpec(memory_space=pltpu.HBM)
    copies = adjoint.shape[1] + 1
    return pl.pallas_call(
        deliver_kernel,
        out_shape=tuple(jax.ShapeDtypeStruct(v.shape, v.dtype) for v in (adjoint, gradient)),
        in_specs=[far, far],
        out_specs=(far, far),
        scratch_shapes=[
            pltpu.VMEM(adjoint.shape, adjoint.dtype),
            pltpu.VMEM(gradient.shape, gradient.dtype),
            pltpu.SemaphoreType.DMA((copies,)),
            pltpu.SemaphoreType.DMA((copies,)),
        ],
        compiler_params=pltpu.CompilerParams(vmem_limit_bytes=60 << 20),
    )(adjoint, gradient)


def body(
    adjoint_in,
    forward_terms,
    log_conductivity,
    spacing,
    residuals,
    gate_index,
    counts,
    voxel_column,
    voxel_model,
):
    tile_count = lax.axis_size("tx")
    adjoint, sensitivity, regularity = field_phase(
        tile_count,
        adjoint_in,
        forward_terms,
        log_conductivity,
        spacing,
        residuals,
        gate_index,
        counts,
        voxel_model,
    )
    gradient = relayout(tile_count, sensitivity, voxel_column, regularity)
    return deliver(adjoint, gradient)


def solution(mesh):
    in_specs = (
        P(None, ("grp", "tx"), None, None),
        P(None, None, ("grp", "tx"), None, None),
        P(("grp", "tx"), None, None),
        P(("grp", "tx"), None),
        P(None, ("grp", "tx"), None),
        P("grp"),
        P(("grp", "tx"), None),
        P(("grp", "tx"), None),
        P(("grp", "tx"), None, None),
    )
    out_specs = (P(None, ("grp", "tx"), None, None), P(("grp", "tx"), None, None))
    return jax.shard_map(body, mesh=mesh, in_specs=in_specs, out_specs=out_specs, check_vma=False)
```
